128 devices in a mesh: dp: 4 (over z_hi, core), ctx: 32 (over z_lo, x, y).
Axes of the slice: x: 4, y: 4, z: 4 (z_hi: 2, z_lo: 2; z = z_hi * 2 + z_lo), core: 2. Of those that a mesh axis runs over, the one named last changes fastest.
Arguments:
- series: bfloat16 [4, 16384, 512], P('dp', 'ctx'), may hold values from -12 to 12
- w_query: bfloat16 [512, 512], replicated, may hold values from -0.375 to 0.375
- w_key: bfloat16 [512, 512], replicated, may hold values from -0.375 to 0.375
- w_value: bfloat16 [512, 512], replicated, may hold values from -0.25 to 0.25
- w_out: bfloat16 [512, 512], replicated, may hold values from -0.25 to 0.25
- cotangent: bfloat16 [4, 16384, 512], P('dp', 'ctx'), may hold values from -6 to 6
Outputs:
- output: bfloat16 [4, 16384, 512], P('dp', 'ctx')
- input_grad: bfloat16 [4, 16384, 512], P('dp', 'ctx')
- grad_query: float32 [512, 512], P(None, ('dp', 'ctx'))
- grad_key: float32 [512, 512], P(None, ('dp', 'ctx'))
- grad_value: float32 [512, 512], P(None, ('dp', 'ctx'))
- grad_out: float32 [512, 512], P(None, ('dp', 'ctx'))
The draws below stay inside these ranges and needn't reach their ends.
All inputs are finite; a program needn't handle non-finite values.
Results may differ from the reference program's by a relative error of at most 0.034.
Values may be sent and summed in bfloat16 or wider, within the bound.
No kernel may reach another device: no remote copies, remote signals or barrier semaphores. Data moves between devices by JAX's collectives and lax.ppermute only.
A program may use at most 192 MiB of HBM per device.

```python
import math
import jax
import jax.numpy as jnp
from jax import lax

D = 512
HEADS = 8
ROWS = 512
SEQ = 16384
N_DP = 4
N_CTX = 32


def draw_series(key, part):
    key = jax.random.fold_in(key, 11)
    first, second = jax.random.split(key, 2)
    shape = (N_DP, SEQ, D)
    base = jax.random.normal(first, shape, jnp.float32)
    level = 0.35 * jnp.exp(jax.random.uniform(second, (N_DP, SEQ, 1), jnp.float32, -0.5, 0.5))
    values = jnp.clip(base * level, -8.0, 8.0)
    return values.astype(jnp.bfloat16)


def raised(values, key, source, target, parts, factor):
    def block_of(position):
        return (jnp.arange(values.shape[position]) // (values.shape[position] // parts)).reshape((-1,) + (1,) * (values.ndim - 1 - position))

    first = jax.random.permutation(key, parts)[block_of(target)]
    second = (block_of(target) + parts // 2) % parts
    return jnp.where((block_of(source) == first) | (block_of(source) == second), factor * values, values)


def block_scale(own_key, shape, pieces, low, largest):
    def one(dim, blocks):
        draws = jax.random.uniform(jax.random.fold_in(jax.random.fold_in(own_key, 6), dim), (blocks,), jnp.float32, low / len(pieces), largest / len(pieces))
        return jnp.repeat(jnp.exp(draws), shape[dim] // blocks).reshape((-1,) + (1,) * (len(shape) - dim - 1))

    factor_of = one(*pieces[0])
    for cut in pieces[1:]:
        factor_of = factor_of * one(*cut)
    return factor_of


def centred(rng, shape, scale, most, cuts=(), kind=jnp.bfloat16):
    gain = block_scale(rng, shape, cuts, -0.22, 0.18) if cuts else 1.0
    drawn = jax.random.normal(rng, shape, jnp.float32) * scale * gain
    return jnp.minimum(jnp.maximum(drawn, -most), most).astype(kind)


def noise_with(stream_key, extent, width, bound, pieces, heavy, held_as=jnp.bfloat16):
    values = width * jax.random.normal(stream_key, extent, jnp.float32)
    if pieces:
        values = values * block_scale(stream_key, extent, pieces, -0.22, 0.18)
    return jnp.clip(raised(values, jax.random.fold_in(stream_key, 3), *heavy), -bound, bound).astype(held_as)


def setup_inputs(seed: int = 0) -> dict:
    splits = jax.random.split(jax.random.key(seed), 7)
    series = draw_series(jax.random.fold_in(splits[6], 71), 0)
    w_query = centred(splits[1], (D, D), (D // 2) ** -0.5, 0.375)
    w_key = centred(splits[2], (D, D), (D // 2) ** -0.5, 0.375)
    w_value = centred(splits[3], (D, D), D ** -0.5, 0.25)
    w_out = centred(splits[4], (D, D), D ** -0.5, 0.25)
    cotangent = noise_with(splits[5], (N_DP, SEQ, D), 1.0, 6.0, ((0, 4), (1, 32)), (1, 2, 32, 2.75))
    return {"series": series, "w_query": w_query, "w_key": w_key, "w_value": w_value, "w_out": w_out, "cotangent": cotangent}


def head_split(block):
    return block.astype(jnp.float32).reshape(block.shape[0], HEADS, D // HEADS).transpose(1, 0, 2)

def merge_heads(block):
    return block.transpose(1, 0, 2).reshape(block.shape[1], D)

def score_block(queries, keys):
    factor = 1.0 / math.sqrt(D // HEADS)
    return jnp.einsum('hqd,hkd->hqk', head_split(queries), head_split(keys)) * factor

def distances():
    found = []
    step = 1
    while step < N_CTX:
        found.append(step)
        step = step * 2
    return found

def reference(series, w_query, w_key, w_value, w_out, cotangent):
    count = N_DP * N_CTX
    factor = 1.0 / math.sqrt(D // HEADS)
    flat = series.reshape(count * ROWS, D)

    def project(weight):
        return jnp.dot(flat, weight, preferred_element_type=jnp.float32).astype(jnp.bfloat16).reshape(count, ROWS, D)
    queries = project(w_query)
    keys = project(w_key)
    values = project(w_value)
    causal = lax.broadcasted_iota(jnp.int32, (1, ROWS, ROWS), 1) >= lax.broadcasted_iota(jnp.int32, (1, ROWS, ROWS), 2)
    reach = distances()

    def sources(block, upward):
        shard = block % N_CTX
        found = [(block, causal)]
        for step in reach:
            if upward:
                valid = shard + step < N_CTX
                other = jnp.where(valid, block + step, block).astype(jnp.int32)
            else:
                valid = shard >= step
                other = jnp.where(valid, block - step, block).astype(jnp.int32)
            found.append((other, valid))
        return found

    def forward_block(block):
        listed = sources(block, False)
        scores = [jnp.where(valid, score_block(queries[block], keys[other]), -jnp.inf) for other, valid in listed]
        log_totals = jax.nn.logsumexp(jnp.concatenate(scores, axis=2), axis=2)
        mixed = jnp.zeros((HEADS, ROWS, D // HEADS), jnp.float32)
        for (other, valid), part in zip(listed, scores):
            weights = jnp.exp(part - log_totals[:, :, None]).astype(jnp.bfloat16)
            mixed = mixed + jnp.einsum('hqk,hkd->hqd', weights.astype(jnp.float32), head_split(values[other]))
        return (log_totals, merge_heads(mixed))
    blocks = jnp.arange(count, dtype=jnp.int32)
    log_totals, mixed = lax.map(forward_block, blocks)
    attended = mixed.astype(jnp.bfloat16)
    attended_flat = attended.reshape(count * ROWS, D)
    output = jnp.dot(attended_flat, w_out, preferred_element_type=jnp.float32).astype(jnp.bfloat16)
    upstream = cotangent.reshape(count * ROWS, D)
    out_grads = jnp.dot(upstream, w_out.T, preferred_element_type=jnp.float32).astype(jnp.bfloat16).reshape(count, ROWS, D)
    products = out_grads.astype(jnp.float32) * attended.astype(jnp.float32)
    row_deltas = lax.optimization_barrier(jnp.sum(products.reshape(count, ROWS, HEADS, D // HEADS), axis=3)).transpose(0, 2, 1)

    def terms(query_block, key_block, allowed):
        scores = jnp.where(allowed, score_block(queries[query_block], keys[key_block]), -jnp.inf)
        weights = jnp.exp(scores - log_totals[query_block][:, :, None])
        weight_grads = jnp.einsum('hqd,hkd->hqk', head_split(out_grads[query_block]), head_split(values[key_block]))
        score_grads = (weights * (weight_grads - row_deltas[query_block][:, :, None])).astype(jnp.bfloat16)
        return (weights.astype(jnp.bfloat16), score_grads)

    def query_side(block):
        total = jnp.zeros((HEADS, ROWS, D // HEADS), jnp.float32)
        for other, valid in sources(block, False):
            weights, score_grads = terms(block, other, valid)
            total = total + jnp.einsum('hqk,hkd->hqd', score_grads.astype(jnp.float32), head_split(keys[other]))
        return merge_heads(total * factor)

    def key_side(block):
        key_total = jnp.zeros((HEADS, ROWS, D // HEADS), jnp.float32)
        value_total = jnp.zeros((HEADS, ROWS, D // HEADS), jnp.float32)
        for other, valid in sources(block, True):
            weights, score_grads = terms(other, block, valid)
            key_total = key_total + jnp.einsum('hqk,hqd->hkd', score_grads.astype(jnp.float32), head_split(queries[other]))
            value_total = value_total + jnp.einsum('hqk,hqd->hkd', weights.astype(jnp.float32), head_split(out_grads[other]))
        return (merge_heads(key_total * factor), merge_heads(value_total))
    query_grad = lax.map(query_side, blocks).astype(jnp.bfloat16).reshape(count * ROWS, D)
    key_total, value_total = lax.map(key_side, blocks)
    key_grad = key_total.astype(jnp.bfloat16).reshape(count * ROWS, D)
    value_grad = value_total.astype(jnp.bfloat16).reshape(count * ROWS, D)
    input_grad = (jnp.dot(query_grad, w_query.T, preferred_element_type=jnp.float32) + jnp.dot(key_grad, w_key.T, preferred_element_type=jnp.float32) + jnp.dot(value_grad, w_value.T, preferred_element_type=jnp.float32)).astype(jnp.bfloat16)
    grad_query = jnp.dot(flat.T, query_grad, preferred_element_type=jnp.float32)
    grad_key = jnp.dot(flat.T, key_grad, preferred_element_type=jnp.float32)
    grad_value = jnp.dot(flat.T, value_grad, preferred_element_type=jnp.float32)
    grad_out = jnp.dot(attended_flat.T, upstream, preferred_element_type=jnp.float32)
    return (output.reshape(N_DP, SEQ, D), input_grad.reshape(N_DP, SEQ, D), grad_query, grad_key, grad_value, grad_out)
```

```python
import functools

import jax
import jax.numpy as jnp
from jax import lax
from jax.experimental import pallas as pl
from jax.experimental.pallas import tpu as pltpu
from jax.sharding import PartitionSpec as P

HEADS = 8
SIZE = 64
F32 = jnp.float32
BF16 = jnp.bfloat16
LOW = -3.0e38
CHUNK = 256
MIB = 2**20


def dot(left, right, left_dim, right_dim):
    return lax.dot_general(
        left, right, (((left_dim,), (right_dim,)), ((), ())), preferred_element_type=F32
    )


def whole(shape):
    return pl.BlockSpec(shape, lambda *_: (0,) * len(shape))


def head_rows(width):
    return pl.BlockSpec((SIZE, width), lambda h: (h, 0))


def head_stat(width):
    return pl.BlockSpec((1, 1, width), lambda h: (h, 0, 0))


SCALAR = pl.BlockSpec(memory_space=pltpu.SMEM)


def params(mib=16):
    return pltpu.CompilerParams(vmem_limit_bytes=mib * MIB)


def cost(matmuls, nbytes=0, exps=0):
    return pl.CostEstimate(
        flops=int(matmuls * 2**24), bytes_accessed=int(nbytes) // 8, transcendentals=0
    )


def project_kernel(x_ref, cot_ref, wq_ref, wo_ref, q_ref, do_ref):
    q_ref[...] = dot(wq_ref[...], x_ref[...], 1, 1).astype(BF16) * jnp.asarray(0.125, BF16)
    do_ref[...] = dot(wo_ref[...], cot_ref[...], 1, 1).astype(BF16)


def project(x, cot, wq_t, w_out):
    n, d = x.shape
    return pl.pallas_call(
        project_kernel,
        out_shape=(jax.ShapeDtypeStruct((d, n), BF16), jax.ShapeDtypeStruct((d, n), BF16)),
        compiler_params=params(),
        cost_estimate=cost(2 * 4),
        name="project",
    )(x, cot, wq_t, w_out)


def forward_kernel(own, seen_ref, x_ref, wk_ref, wv_ref, q_ref, p_ref, m_ref, l_ref, o_ref, k_ref, v_ref):
    head = pl.program_id(0)
    seen = seen_ref[0] > 0

    @pl.when(jnp.logical_and(seen, head == 0))
    def _():
        k_ref[...] = dot(wk_ref[...], x_ref[...], 1, 1).astype(BF16)
        v_ref[...] = dot(wv_ref[...], x_ref[...], 1, 1).astype(BF16)

    @pl.when(seen)
    def _():
        rows = pl.ds(pl.multiple_of(head * SIZE, SIZE), SIZE)
        keys = k_ref[rows, :]
        ones = jnp.ones((16, keys.shape[1]), BF16)
        values = jnp.concatenate([v_ref[rows, :], ones], axis=0)
        for start in range(0, q_ref.shape[1], CHUNK):
            cols = slice(start, start + CHUNK)
            known = min(start + CHUNK, keys.shape[1]) if own else keys.shape[1]
            scores = dot(keys[:, :known], q_ref[:, cols], 0, 0)
            if own:
                at_key = lax.broadcasted_iota(jnp.int32, scores.shape, 0)
                at_query = lax.broadcasted_iota(jnp.int32, scores.shape, 1) + start
                scores = jnp.where(at_key <= at_query, scores, LOW)
            largest = jnp.max(scores, axis=0, keepdims=True)
            weights = jnp.exp(scores - largest).astype(BF16)
            mixed = dot(values[:, :known], weights, 1, 0)
            p_ref[0, :known, cols] = weights
            if known < keys.shape[1]:
                p_ref[0, known:, cols] = jnp.zeros((keys.shape[1] - known, CHUNK), BF16)
            m_ref[0, :, cols] = largest
            l_ref[0, :, cols] = mixed[SIZE : SIZE + 1, :]
            o_ref[:, cols] = mixed[:SIZE, :]

    @pl.when(jnp.logical_not(seen))
    def _():
        m_ref[...] = jnp.full(m_ref.shape, LOW, F32)
        l_ref[...] = jnp.zeros(l_ref.shape, F32)
        o_ref[...] = jnp.zeros(o_ref.shape, F32)


def forward(own, seen, x, wk_t, wv_t, q_t):
    n, d = x.shape
    return pl.pallas_call(
        functools.partial(forward_kernel, own),
        grid=(HEADS,),
        out_shape=(
            jax.ShapeDtypeStruct((HEADS, n, n), BF16),
            jax.ShapeDtypeStruct((HEADS, 1, n), F32),
            jax.ShapeDtypeStruct((HEADS, 1, n), F32),
            jax.ShapeDtypeStruct((d, n), F32),
            jax.ShapeDtypeStruct((d, n), BF16),
            jax.ShapeDtypeStruct((d, n), BF16),
        ),
        in_specs=[SCALAR, whole((n, d)), whole((d, d)), whole((d, d)), head_rows(n)],
        out_specs=[
            pl.BlockSpec((1, n, n), lambda h: (h, 0, 0)),
            head_stat(n),
            head_stat(n),
            head_rows(n),
            whole((d, n)),
            whole((d, n)),
        ],
        compiler_params=params(),
        cost_estimate=cost(2 * 4 + 2, 7 * MIB, HEADS * n * n),
        name="forward_own" if own else "forward_far",
    )(seen, x, wk_t, wv_t, q_t)


def join_kernel(count, *refs):
    ms, ls, os = refs[:count], refs[count : 2 * count], refs[2 * count : 3 * count]
    do_ref, wo_ref, cot_ref = refs[3 * count : 3 * count + 3]
    att_ref, out_ref, delta_ref = refs[3 * count + 3 : 3 * count + 6]
    cs = refs[3 * count + 6 :]
    for head in range(HEADS):
        rows = slice(head * SIZE, (head + 1) * SIZE)
        largest = functools.reduce(jnp.maximum, [m[head] for m in ms])
        factors = [jnp.exp(m[head] - largest) for m in ms]
        total = functools.reduce(jnp.add, [f * l[head] for f, l in zip(factors, ls)])
        inverse = 1.0 / total
        mixed = None
        for f, o, c in zip(factors, os, cs):
            f = f * inverse
            c[head] = f
            term = o[rows, :] * f
            mixed = term if mixed is None else mixed + term
        attended = mixed.astype(BF16)
        att_ref[rows, :] = attended
        products = attended.astype(F32) * do_ref[rows, :].astype(F32)
        delta_ref[head] = jnp.sum(products, axis=0, keepdims=True)
    out_ref[...] = dot(att_ref[...], wo_ref[...], 0, 0).astype(BF16)


def join(stats, do_t, w_out, cot):
    d, n = do_t.shape
    count = len(stats)
    row = jax.ShapeDtypeStruct((HEADS, 1, n), F32)
    return pl.pallas_call(
        functools.partial(join_kernel, count),
        out_shape=(
            jax.ShapeDtypeStruct((d, n), BF16),
            jax.ShapeDtypeStruct((n, d), BF16),
            row,
        )
        + (row,) * count,
        compiler_params=params(),
        cost_estimate=cost(4, 8 * MIB),
        name="join",
    )(*[s[0] for s in stats], *[s[1] for s in stats], *[s[2] for s in stats], do_t, w_out, cot)


def backward_kernel(
    last, carried, seen_ref, p_ref, k_ref, v_ref, q_ref, do_ref, c_ref, delta_ref, wk_ref, wv_ref, wq_ref, acc_ref,
    *rest,
):
    carry_refs, rest = rest[:carried], rest[carried:]
    dq_ref, dk_ref, dv_ref, dx_ref, *scratch = rest
    head = pl.program_id(0)
    seen = seen_ref[0] > 0

    @pl.when(seen)
    def _():
        rows = pl.ds(pl.multiple_of(head * SIZE, SIZE), SIZE)
        keys = k_ref[...]
        values = v_ref[...]
        factor = c_ref[0]
        scaled_q = (q_ref[...].astype(F32) * factor).astype(BF16)
        scaled_do = (do_ref[...].astype(F32) * factor).astype(BF16)
        dk = jnp.zeros(keys.shape, F32)
        dv = jnp.zeros(keys.shape, F32)
        for start in range(0, q_ref.shape[1], CHUNK):
            cols = slice(start, start + CHUNK)
            weights = p_ref[0, :, cols]
            grads = dot(values, do_ref[:, cols], 0, 0) - delta_ref[0, :, cols]
            grads = weights * grads.astype(BF16)
            dq_ref[:, cols] = acc_ref[:, cols] + dot(keys, grads, 1, 0) * factor[:, cols]
            dk = dk + dot(scaled_q[:, cols], grads, 1, 1)
            dv = dv + dot(scaled_do[:, cols], weights, 1, 1)
        dk_ref[rows, :] = dk.astype(BF16)
        dv_ref[rows, :] = dv.astype(BF16)
        if last:
            (all_dq,) = scratch
            all_dq[rows, :] = (dq_ref[...] * 0.125).astype(BF16)

    @pl.when(jnp.logical_not(seen))
    def _():
        rows = pl.ds(pl.multiple_of(head * SIZE, SIZE), SIZE)
        dq_ref[...] = acc_ref[...]
        dk_ref[rows, :] = jnp.zeros(k_ref.shape, BF16)
        dv_ref[rows, :] = jnp.zeros(k_ref.shape, BF16)

    @pl.when(head == HEADS - 1)
    def _():
        total = dot(dk_ref[...], wk_ref[...], 0, 0) + dot(dv_ref[...], wv_ref[...], 0, 0)
        if last:
            (all_dq,) = scratch
            total = total + dot(all_dq[...], wq_ref[...], 0, 0)
        for place, carry_ref in enumerate(carry_refs):
            total = total + jnp.where(seen_ref[1 + place] > 0, carry_ref[...], 0).astype(F32)
        dx_ref[...] = total.astype(dx_ref.dtype)


def backward(last, seen, p, k, v, q_t, do_t, c, delta, wk_t, wv_t, wq_t, acc, *carry):
    d, n = q_t.shape
    return pl.pallas_call(
        functools.partial(backward_kernel, last, len(carry)),
        grid=(HEADS,),
        out_shape=(
            jax.ShapeDtypeStruct((d, n), F32),
            jax.ShapeDtypeStruct((d, n), BF16),
            jax.ShapeDtypeStruct((d, n), BF16),
            jax.ShapeDtypeStruct((n, d), F32 if last else BF16),
        ),
        in_specs=[
            SCALAR,
            pl.BlockSpec((1, n, n), lambda h: (h, 0, 0)),
            head_rows(n),
            head_rows(n),
            head_rows(n),
            head_rows(n),
            head_stat(n),
            head_stat(n),
            whole((d, d)),
            whole((d, d)),
            whole((d, d)),
            head_rows(n),
        ]
        + [whole((n, d))] * len(carry),
        out_specs=[head_rows(n), whole((d, n)), whole((d, n)), whole((n, d))],
        scratch_shapes=[pltpu.VMEM((d, n), BF16)] if last else [],
        compiler_params=params(),
        cost_estimate=cost(4 * 4 + 2, 10 * MIB),
        name="backward_own" if last else "backward_far",
    )(seen, p, k, v, q_t, do_t, c, delta, wk_t, wv_t, wq_t, acc, *carry)


def weights_kernel(count, *refs):
    xs, dks, dvs = refs[:count], refs[count : 2 * count], refs[2 * count : 3 * count]
    dq_ref, att_ref, cot_ref, g_ref, sums = refs[3 * count :]

    def keep(place, value):
        for owner in range(g_ref.shape[0]):
            sums[owner, 4 * place : 4 * place + 4, :] = value[4 * owner : 4 * owner + 4, :]

    keep(0, dot((dq_ref[...] * 0.125).astype(BF16), xs[0][...], 1, 0))
    for place, parts in ((1, dks), (2, dvs)):
        total = None
        for part, x in zip(parts, xs):
            term = dot(part[...], x[...], 1, 0)
            total = term if total is None else total + term
        keep(place, total)
    keep(3, dot(cot_ref[...], att_ref[...], 0, 1))
    g_ref[...] = sums[...].astype(BF16)


def weight_terms(xs, dks, dvs, dq, att_t, cot):
    n, d = cot.shape
    return pl.pallas_call(
        functools.partial(weights_kernel, len(xs)),
        out_shape=jax.ShapeDtypeStruct((128, 16, d), BF16),
        scratch_shapes=[pltpu.VMEM((128, 16, d), F32)],
        compiler_params=params(32),
        cost_estimate=cost(2 * len(xs) + 2, 12 * MIB),
        name="weight_terms",
    )(*xs, *dks, *dvs, dq, att_t, cot)


def place(z, x, y):
    return (z % 2) * 16 + (x % 4) * 4 + y % 4


def y_ring(value, step):
    pairs = [(place(z, x, y), place(z, x, y + step)) for z in range(2) for x in range(4) for y in range(4)]
    return lax.ppermute(value, "ctx", pairs)


def shifted(value, step):
    return lax.ppermute(
        value, "ctx", [(i, i + step) for i in range(max(0, -step), min(32, 32 - step))]
    )


def body(series, w_query, w_key, w_value, w_out, cotangent):
    x = series[0]
    cot = cotangent[0]
    n, d = x.shape
    position = lax.axis_index("ctx")
    y = position % 4
    x4, x8, x16 = shifted(x, 4), shifted(x, 8), shifted(x, 16)
    wq_t, wk_t, wv_t = w_query.T, w_key.T, w_value.T
    q_t, do_t = project(x, cot, wq_t, w_out)
    order = (0, 4, 16, 8, 1, 2)
    seen = {p: (position >= p).astype(jnp.int32).reshape(1) for p in order}
    held = {0: forward(True, seen[0], x, wk_t, wv_t, q_t)}
    x4, _ = lax.optimization_barrier((x4, held[0][1]))
    x1 = y_ring(jnp.where(y == 3, x4, x), 1)
    x2 = y_ring(jnp.where(y >= 2, x4, x), 2)
    blocks = {0: x, 1: x1, 2: x2, 4: x4, 8: x8, 16: x16}
    for p in order[1:]:
        held[p] = forward(False, seen[p], blocks[p], wk_t, wv_t, q_t)
    att_t, output, delta, *factors = join([held[p][1:4] for p in order], do_t, w_out, cot)
    factor = dict(zip(order, factors))
    dq = jnp.zeros((d, n), F32)
    dk, dv, dx = {}, {}, {}
    back = {}
    for p in (1, 2, 8, 16, 4, 0):
        weights, _, _, _, keys, values = held[p]
        flags, carry = seen[p], ()
        if p == 4:
            wraps = jnp.stack([y == 3, y >= 2]).astype(jnp.int32)
            flags, carry = jnp.concatenate([flags, wraps]), (back[1], back[2])
        dq, dk[p], dv[p], dx[p] = backward(
            p == 0, flags, weights, keys, values, q_t, do_t, factor[p], delta, wk_t, wv_t, wq_t, dq, *carry
        )
        if p in (1, 2):
            back[p] = y_ring(dx[p], -p)
        elif p:
            back[p] = shifted(dx[p], -p)
    terms = weight_terms(
        [blocks[p] for p in order], [dk[p] for p in order], [dv[p] for p in order], dq, att_t, cot
    )
    terms, back[4], back[8], back[16] = lax.optimization_barrier((terms, back[4], back[8], back[16]))
    terms = lax.all_to_all(terms, ("dp", "ctx"), 0, 0, tiled=True)
    grads = jnp.sum(terms.astype(F32), axis=0).reshape(4, 4, d).transpose(0, 2, 1)
    total = dx[0] + back[8].astype(F32) + back[16].astype(F32) + back[4].astype(F32)
    total = total + jnp.where(y < 3, back[1], 0).astype(F32) + jnp.where(y < 2, back[2], 0).astype(F32)
    input_grad = total.astype(BF16)
    return (output[None], input_grad[None], grads[0], grads[1], grads[2], grads[3])


def solution(mesh):
    return jax.shard_map(
        body,
        mesh=mesh,
        in_specs=(P("dp", "ctx", None), P(), P(), P(), P(), P("dp", "ctx", None)),
        out_specs=(
            P("dp", "ctx", None),
            P("dp", "ctx", None),
            P(None, ("dp", "ctx")),
            P(None, ("dp", "ctx")),
            P(None, ("dp", "ctx")),
            P(None, ("dp", "ctx")),
        ),
        check_vma=False,
    )
```

```python
import functools

import jax
import jax.numpy as jnp
from jax import lax
from jax.experimental import pallas as pl
from jax.experimental.pallas import tpu as pltpu
from jax.sharding import PartitionSpec as P

HEADS = 8
SIZE = 64
F32 = jnp.float32
BF16 = jnp.bfloat16
LOW = -3.0e38
MIB = 2**20


def dot(left, right, left_dim, right_dim):
    return lax.dot_general(
        left, right, (((left_dim,), (right_dim,)), ((), ())), preferred_element_type=F32
    )


def whole(shape):
    return pl.BlockSpec(shape, lambda *_: (0,) * len(shape), pipeline_mode=pl.Buffered(1))


def head_rows(count, width):
    return pl.BlockSpec((count * SIZE, width), lambda h: (h, 0))


def head_stat(count, width):
    return pl.BlockSpec((count, 1, width), lambda h: (h, 0, 0))


SCALAR = pl.BlockSpec(memory_space=pltpu.SMEM)


def params(mib=16):
    return pltpu.CompilerParams(vmem_limit_bytes=mib * MIB)


def cost(microseconds):
    return pl.CostEstimate(flops=int(microseconds * 1.1e9), bytes_accessed=MIB, transcendentals=0)


def project_kernel(*refs):
    given, outs, scratch = refs[:6], refs[6:11], refs[11:]
    q_ref, do_ref, wq_t_ref, wk_t_ref, wv_t_ref = outs
    held, sems = scratch[:6], scratch[6]
    copies = [pltpu.make_async_copy(a, b, sems.at[i]) for i, (a, b) in enumerate(zip(given, held))]
    for copy in copies:
        copy.start()
    wo, cot, wq, x, wk, wv = held
    copies[0].wait()
    copies[1].wait()
    do_ref[...] = dot(wo[...], cot[...], 1, 1).astype(BF16)
    copies[2].wait()
    wq_t_ref[...] = wq[...].T
    copies[3].wait()
    q_ref[...] = dot(wq_t_ref[...], x[...], 1, 1).astype(BF16) * jnp.asarray(0.125, BF16)
    copies[4].wait()
    wk_t_ref[...] = wk[...].T
    copies[5].wait()
    wv_t_ref[...] = wv[...].T


def project(x, cot, w_query, w_key, w_value, w_out):
    n, d = x.shape
    square = jax.ShapeDtypeStruct((d, d), BF16)
    given = (w_out, cot, w_query, x, w_key, w_value)
    return pl.pallas_call(
        project_kernel,
        out_shape=(jax.ShapeDtypeStruct((d, n), BF16),) * 2 + (square,) * 3,
        in_specs=[pl.BlockSpec(memory_space=pltpu.HBM)] * 6,
        scratch_shapes=[pltpu.VMEM(a.shape, BF16) for a in given] + [pltpu.SemaphoreType.DMA((6,))],
        compiler_params=params(12),
        cost_estimate=cost(2.5),
        name="project",
    )(*given)


def forward_kernel(own, count, seen_ref, x_ref, wk_ref, wv_ref, q_ref, p_ref, m_ref, l_ref, o_ref, k_ref, v_ref):
    step = pl.program_id(0)
    seen = seen_ref[0] > 0

    @pl.when(jnp.logical_and(seen, step == 0))
    def _():
        k_ref[...] = dot(wk_ref[...], x_ref[...], 1, 1).astype(BF16)
        v_ref[...] = dot(wv_ref[...], x_ref[...], 1, 1).astype(BF16)

    @pl.when(seen)
    def _():
        n = q_ref.shape[1]
        chunk = n // 2 if own else n
        parts = [(j, start) for j in range(count) for start in range(0, n, chunk)]
        scores = []
        for j, start in parts:
            known = start + chunk if own else n
            keys = k_ref[pl.ds(pl.multiple_of((step * count + j) * SIZE, SIZE), SIZE), :known]
            scores.append(dot(keys, q_ref[j * SIZE : (j + 1) * SIZE, start : start + chunk], 0, 0))
        for (j, start), score in zip(parts, scores):
            known = start + chunk if own else n
            cols = slice(start, start + chunk)
            if own:
                at_key = lax.broadcasted_iota(jnp.int32, score.shape, 0)
                at_query = lax.broadcasted_iota(jnp.int32, score.shape, 1) + start
                score = jnp.where(at_key <= at_query, score, LOW)
            largest = jnp.max(score, axis=0, keepdims=True)
            weights = jnp.exp(score - largest).astype(BF16)
            p_ref[j, :known, cols] = weights
            if known < n:
                p_ref[j, known:, cols] = jnp.zeros((n - known, chunk), BF16)
            values = v_ref[pl.ds(pl.multiple_of((step * count + j) * SIZE, SIZE), SIZE), :known]
            values = jnp.concatenate([values, jnp.ones((16, known), BF16)], axis=0)
            mixed = dot(values, weights, 1, 0)
            m_ref[j, :, cols] = largest
            l_ref[j, :, cols] = mixed[SIZE : SIZE + 1, :]
            o_ref[j * SIZE : (j + 1) * SIZE, cols] = mixed[:SIZE, :]

    @pl.when(jnp.logical_not(seen))
    def _():
        m_ref[...] = jnp.full(m_ref.shape, LOW, F32)
        l_ref[...] = jnp.zeros(l_ref.shape, F32)
        o_ref[...] = jnp.zeros(o_ref.shape, F32)


def forward(own, seen, x, wk_t, wv_t, q_t):
    n, d = x.shape
    count = 4 if own else 2
    return pl.pallas_call(
        functools.partial(forward_kernel, own, count),
        grid=(HEADS // count,),
        out_shape=(
            jax.ShapeDtypeStruct((HEADS, n, n), BF16),
            jax.ShapeDtypeStruct((HEADS, 1, n), F32),
            jax.ShapeDtypeStruct((HEADS, 1, n), F32),
            jax.ShapeDtypeStruct((d, n), F32),
            jax.ShapeDtypeStruct((d, n), BF16),
            jax.ShapeDtypeStruct((d, n), BF16),
        ),
        in_specs=[SCALAR, whole((n, d)), whole((d, d)), whole((d, d)), head_rows(count, n)],
        out_specs=[
            pl.BlockSpec((count, n, n), lambda h: (h, 0, 0)),
            head_stat(count, n),
            head_stat(count, n),
            head_rows(count, n),
            whole((d, n)),
            whole((d, n)),
        ],
        compiler_params=params(11),
        cost_estimate=cost(4.5 if own else 6),
        name="forward_own" if own else "forward_far",
    )(seen, x, wk_t, wv_t, q_t)


def join_kernel(count, *refs):
    ms, ls, os = refs[:count], refs[count : 2 * count], refs[2 * count : 3 * count]
    do_ref, wo_ref, cot_ref = refs[3 * count : 3 * count + 3]
    att_ref, out_ref, delta_ref = refs[3 * count + 3 : 3 * count + 6]
    cs = refs[3 * count + 6 :]
    for head in range(HEADS):
        rows = slice(head * SIZE, (head + 1) * SIZE)
        largest = functools.reduce(jnp.maximum, [m[head] for m in ms])
        factors = [jnp.exp(m[head] - largest) for m in ms]
        total = functools.reduce(jnp.add, [f * l[head] for f, l in zip(factors, ls)])
        inverse = 1.0 / total
        mixed = None
        for f, o, c in zip(factors, os, cs):
            f = f * inverse
            c[head] = f
            term = o[rows, :] * f
            mixed = term if mixed is None else mixed + term
        attended = mixed.astype(BF16)
        att_ref[rows, :] = attended
        products = attended.astype(F32) * do_ref[rows, :].astype(F32)
        delta_ref[head] = jnp.sum(products, axis=0, keepdims=True)
    out_ref[...] = dot(att_ref[...], wo_ref[...], 0, 0).astype(BF16)


def join(stats, do_t, w_out, cot):
    d, n = do_t.shape
    count = len(stats)
    row = jax.ShapeDtypeStruct((HEADS, 1, n), F32)
    return pl.pallas_call(
        functools.partial(join_kernel, count),
        out_shape=(
            jax.ShapeDtypeStruct((d, n), BF16),
            jax.ShapeDtypeStruct((n, d), BF16),
            row,
        )
        + (row,) * count,
        compiler_params=params(),
        cost_estimate=cost(2),
        name="join",
    )(*[s[0] for s in stats], *[s[1] for s in stats], *[s[2] for s in stats], do_t, w_out, cot)


def backward_kernel(
    last, carried, seen_ref, p_ref, k_ref, v_ref, q_ref, do_ref, c_ref, delta_ref, wk_ref, wv_ref, wq_ref, acc_ref,
    *rest,
):
    carry_refs, rest = rest[:carried], rest[carried:]
    dq_ref, dk_ref, dv_ref, dx_ref, *scratch = rest
    step = pl.program_id(0)
    count = p_ref.shape[0]
    seen = seen_ref[0] > 0

    @pl.when(seen)
    def _():
        grads = []
        for j in range(count):
            rows = slice(j * SIZE, (j + 1) * SIZE)
            value_dots = dot(v_ref[rows, :], do_ref[rows, :], 0, 0)
            grads.append(p_ref[j] * (value_dots - delta_ref[j]).astype(BF16))
        for j in range(count):
            rows = slice(j * SIZE, (j + 1) * SIZE)
            out = pl.ds(pl.multiple_of((step * count + j) * SIZE, SIZE), SIZE)
            factor = c_ref[j]
            scaled_q = (q_ref[rows, :].astype(F32) * factor).astype(BF16)
            scaled_do = (do_ref[rows, :].astype(F32) * factor).astype(BF16)
            dq = acc_ref[rows, :] + dot(k_ref[rows, :], grads[j], 1, 0) * factor
            dq_ref[rows, :] = dq
            dk_ref[out, :] = dot(scaled_q, grads[j], 1, 1).astype(BF16)
            dv_ref[out, :] = dot(scaled_do, p_ref[j], 1, 1).astype(BF16)
            if last:
                scratch[0][out, :] = (dq * 0.125).astype(BF16)

    @pl.when(jnp.logical_not(seen))
    def _():
        out = pl.ds(pl.multiple_of(step * count * SIZE, count * SIZE), count * SIZE)
        dq_ref[...] = acc_ref[...]
        dk_ref[out, :] = jnp.zeros(k_ref.shape, BF16)
        dv_ref[out, :] = jnp.zeros(k_ref.shape, BF16)

    @pl.when(step == HEADS // count - 1)
    def _():
        total = dot(dk_ref[...], wk_ref[...], 0, 0) + dot(dv_ref[...], wv_ref[...], 0, 0)
        if last:
            total = total + dot(scratch[0][...], wq_ref[...], 0, 0)
        for place, carry_ref in enumerate(carry_refs):
            total = total + jnp.where(seen_ref[1 + place] > 0, carry_ref[...], 0).astype(F32)
        dx_ref[...] = total.astype(dx_ref.dtype)


def backward(last, seen, p, k, v, q_t, do_t, c, delta, wk_t, wv_t, wq_t, acc, *carry):
    d, n = q_t.shape
    count = 4
    return pl.pallas_call(
        functools.partial(backward_kernel, last, len(carry)),
        grid=(HEADS // count,),
        out_shape=(
            jax.ShapeDtypeStruct((d, n), F32),
            jax.ShapeDtypeStruct((d, n), BF16),
            jax.ShapeDtypeStruct((d, n), BF16),
            jax.ShapeDtypeStruct((n, d), F32 if last else BF16),
        ),
        in_specs=[
            SCALAR,
            pl.BlockSpec((count, n, n), lambda h: (h, 0, 0)),
            *[head_rows(count, n)] * 4,
            *[head_stat(count, n)] * 2,
            *[whole((d, d))] * 3,
            head_rows(count, n),
        ]
        + [whole((n, d))] * len(carry),
        out_specs=[head_rows(count, n), whole((d, n)), whole((d, n)), whole((n, d))],
        scratch_shapes=[pltpu.VMEM((d, n), BF16)] if last else [],
        compiler_params=params(13),
        cost_estimate=cost(5.5),
        name="backward_own" if last else "backward_far",
    )(seen, p, k, v, q_t, do_t, c, delta, wk_t, wv_t, wq_t, acc, *carry)


def added(parts, xs, total=None):
    for part, x in zip(parts, xs):
        term = dot(part[...], x[...], 1, 0)
        total = term if total is None else total + term
    return total


def early_kernel(count, *refs):
    xs, dks, dvs = refs[:count], refs[count : 2 * count], refs[2 * count : 3 * count]
    att_ref, cot_ref, g_ref = refs[3 * count :]
    g_ref[0] = added(dks, xs)
    g_ref[1] = added(dvs, xs)
    g_ref[2] = dot(cot_ref[...], att_ref[...], 0, 1)


def early_terms(xs, dks, dvs, att_t, cot):
    n, d = cot.shape
    return pl.pallas_call(
        functools.partial(early_kernel, len(xs)),
        out_shape=jax.ShapeDtypeStruct((3, d, d), F32),
        compiler_params=params(14),
        cost_estimate=cost(4),
        name="early_terms",
    )(*xs, *dks, *dvs, att_t, cot)


def weights_kernel(count, core_ref, *refs):
    xs, dks, dvs = refs[:count], refs[count : 2 * count], refs[2 * count : 3 * count]
    dq_ref, early_ref, keep_ref, give_ref, sums = refs[3 * count :]

    def keep(place, value):
        for owner in range(sums.shape[0]):
            sums[owner, 4 * place : 4 * place + 4, :] = value[4 * owner : 4 * owner + 4, :]

    keep(0, dot((dq_ref[...] * 0.125).astype(BF16), xs[0][...], 1, 0))
    keep(1, added(dks, xs, early_ref[0]))
    keep(2, added(dvs, xs, early_ref[1]))
    keep(3, early_ref[2])
    core = core_ref[0]
    for high in range(2):
        here = pl.ds(pl.multiple_of((2 * high + core) * 32, 32), 32)
        there = pl.ds(pl.multiple_of((2 * high + 1 - core) * 32, 32), 32)
        keep_ref[32 * high : 32 * high + 32] = sums[here].astype(BF16)
        give_ref[32 * high : 32 * high + 32] = sums[there].astype(BF16)


def weight_terms(core, xs, dks, dvs, dq, early):
    n, d = xs[0].shape
    half = jax.ShapeDtypeStruct((64, 16, d), BF16)
    return pl.pallas_call(
        functools.partial(weights_kernel, len(xs)),
        out_shape=(half, half),
        in_specs=[SCALAR] + [pl.BlockSpec(memory_space=pltpu.VMEM)] * (3 * len(xs) + 2),
        scratch_shapes=[pltpu.VMEM((128, 16, d), F32)],
        compiler_params=params(18),
        cost_estimate=cost(3.5),
        name="weight_terms",
    )(core, *xs, *dks, *dvs, dq, early)


def place(z, x, y):
    return (z % 2) * 16 + (x % 4) * 4 + y % 4


def y_ring(value, step):
    pairs = [(place(z, x, y), place(z, x, y + step)) for z in range(2) for x in range(4) for y in range(4)]
    return lax.ppermute(value, "ctx", pairs)


def shifted(value, step):
    return lax.ppermute(
        value, "ctx", [(i, i + step) for i in range(max(0, -step), min(32, 32 - step))]
    )


def body(series, w_query, w_key, w_value, w_out, cotangent):
    x = series[0]
    cot = cotangent[0]
    n, d = x.shape
    position = lax.axis_index("ctx")
    y = position % 4
    x4 = shifted(x, 4)
    q_t, do_t, wq_t, wk_t, wv_t = project(x, cot, w_query, w_key, w_value, w_out)
    order = (0, 4, 1, 2, 16, 8)
    seen = {p: (position >= p).astype(jnp.int32).reshape(1) for p in order}
    held = {0: forward(True, seen[0], x, wk_t, wv_t, q_t)}
    x4, later, _ = lax.optimization_barrier((x4, x, held[0][1]))
    x1 = y_ring(jnp.where(y == 3, x4, later), 1)
    x2 = y_ring(jnp.where(y >= 2, x4, later), 2)
    x16, x8 = shifted(later, 16), shifted(later, 8)
    blocks = {0: x, 1: x1, 2: x2, 4: x4, 8: x8, 16: x16}
    for p in order[1:]:
        held[p] = forward(False, seen[p], blocks[p], wk_t, wv_t, q_t)
    att_t, output, delta, *factors = join([held[p][1:4] for p in order], do_t, w_out, cot)
    factor = dict(zip(order, factors))
    dq = jnp.zeros((d, n), F32)
    dk, dv, dx = {}, {}, {}
    back = {}
    for p in (1, 2, 8, 16, 4, 0):
        weights, _, _, _, keys, values = held[p]
        flags, carry = seen[p], ()
        if p == 4:
            ready = (1, 2, 8, 16)
            early = early_terms(
                [blocks[i] for i in ready], [dk[i] for i in ready], [dv[i] for i in ready], att_t, cot
            )
            early, back[1], back[2] = lax.optimization_barrier((early, back[1], back[2]))
            wraps = jnp.stack([y == 3, y >= 2]).astype(jnp.int32)
            flags, carry = jnp.concatenate([flags, wraps]), (back[1], back[2])
        dq, dk[p], dv[p], dx[p] = backward(
            p == 0, flags, weights, keys, values, q_t, do_t, factor[p], delta, wk_t, wv_t, wq_t, dq, *carry
        )
        if p in (1, 2):
            back[p] = y_ring(dx[p], -p)
        elif p:
            back[p] = shifted(dx[p], -p)
    core = lax.axis_index("dp") % 2
    kept, given = weight_terms(
        core.astype(jnp.int32).reshape(1), [x, x4], [dk[0], dk[4]], [dv[0], dv[4]], dq, early
    )
    kept, given, back[4], back[8], back[16] = lax.optimization_barrier(
        (kept, given, back[4], back[8], back[16])
    )
    given = lax.ppermute(given, "dp", [(0, 1), (1, 0), (2, 3), (3, 2)])
    terms = (kept.astype(F32) + given.astype(F32)).astype(BF16)
    same_core = [[32 * i + j for i in (k, k + 2) for j in range(32)] for k in range(2)]
    terms = lax.all_to_all(terms, ("dp", "ctx"), 0, 0, axis_index_groups=same_core, tiled=True)
    grads = jnp.sum(terms.astype(F32), axis=0).reshape(4, 4, d).transpose(0, 2, 1)
    total = dx[0] + back[8].astype(F32) + back[16].astype(F32) + back[4].astype(F32)
    total = total + jnp.where(y < 3, back[1], 0).astype(F32) + jnp.where(y < 2, back[2], 0).astype(F32)
    input_grad = total.astype(BF16)
    return (output[None], input_grad[None], grads[0], grads[1], grads[2], grads[3])


def solution(mesh):
    return jax.shard_map(
        body,
        mesh=mesh,
        in_specs=(P("dp", "ctx", None), P(), P(), P(), P(), P("dp", "ctx", None)),
        out_specs=(
            P("dp", "ctx", None),
            P("dp", "ctx", None),
            P(None, ("dp", "ctx")),
            P(None, ("dp", "ctx")),
            P(None, ("dp", "ctx")),
            P(None, ("dp", "ctx")),
        ),
        check_vma=False,
    )
```

```python
import functools

import jax
import jax.numpy as jnp
from jax import lax
from jax.experimental import pallas as pl
from jax.experimental.pallas import tpu as pltpu
from jax.sharding import PartitionSpec as P

HEADS = 8
SIZE = 64
F32 = jnp.float32
BF16 = jnp.bfloat16
LOW = -3.0e38
MIB = 2**20


def dot(left, right, left_dim, right_dim):
    return lax.dot_general(
        left, right, (((left_dim,), (right_dim,)), ((), ())), preferred_element_type=F32
    )


def whole(shape):
    return pl.BlockSpec(shape, lambda *_: (0,) * len(shape), pipeline_mode=pl.Buffered(1))


def head_rows(count, width):
    return pl.BlockSpec((count * SIZE, width), lambda h: (h, 0))


def head_stat(count, width):
    return pl.BlockSpec((count, 1, width), lambda h: (h, 0, 0))


SCALAR = pl.BlockSpec(memory_space=pltpu.SMEM)


def params(mib=16):
    return pltpu.CompilerParams(vmem_limit_bytes=mib * MIB)


def cost(microseconds):
    return pl.CostEstimate(flops=int(microseconds * 1.1e9), bytes_accessed=MIB, transcendentals=0)


def project_kernel(x_ref, wq_ref, wk_ref, wv_ref, q_ref, wq_t_ref, wk_t_ref, wv_t_ref):
    wq_t_ref[...] = wq_ref[...].T
    q_ref[...] = dot(wq_t_ref[...], x_ref[...], 1, 1).astype(BF16) * jnp.asarray(0.125, BF16)
    wk_t_ref[...] = wk_ref[...].T
    wv_t_ref[...] = wv_ref[...].T


def project(x, w_query, w_key, w_value):
    n, d = x.shape
    square = jax.ShapeDtypeStruct((d, d), BF16)
    return pl.pallas_call(
        project_kernel,
        out_shape=(jax.ShapeDtypeStruct((d, n), BF16),) + (square,) * 3,
        compiler_params=params(12),
        cost_estimate=cost(2),
        name="project",
    )(x, w_query, w_key, w_value)


def forward_kernel(own, count, seen_ref, x_ref, wk_ref, wv_ref, q_ref, p_ref, m_ref, l_ref, o_ref, k_ref, v_ref):
    step = pl.program_id(0)
    seen = seen_ref[0] > 0

    @pl.when(jnp.logical_and(seen, step == 0))
    def _():
        k_ref[...] = dot(wk_ref[...], x_ref[...], 1, 1).astype(BF16)
        v_ref[...] = dot(wv_ref[...], x_ref[...], 1, 1).astype(BF16)

    @pl.when(seen)
    def _():
        n = q_ref.shape[1]
        chunk = n // 2 if own else n
        parts = [(j, start) for j in range(count) for start in range(0, n, chunk)]
        scores = []
        for j, start in parts:
            known = start + chunk if own else n
            keys = k_ref[pl.ds(pl.multiple_of((step * count + j) * SIZE, SIZE), SIZE), :known]
            scores.append(dot(keys, q_ref[j * SIZE : (j + 1) * SIZE, start : start + chunk], 0, 0))
        for (j, start), score in zip(parts, scores):
            known = start + chunk if own else n
            cols = slice(start, start + chunk)
            if own:
                at_key = lax.broadcasted_iota(jnp.int32, score.shape, 0)
                at_query = lax.broadcasted_iota(jnp.int32, score.shape, 1) + start
                score = jnp.where(at_key <= at_query, score, LOW)
            largest = jnp.max(score, axis=0, keepdims=True)
            weights = jnp.exp(score - largest).astype(BF16)
            p_ref[j, :known, cols] = weights
            if known < n:
                p_ref[j, known:, cols] = jnp.zeros((n - known, chunk), BF16)
            values = v_ref[pl.ds(pl.multiple_of((step * count + j) * SIZE, SIZE), SIZE), :known]
            values = jnp.concatenate([values, jnp.ones((16, known), BF16)], axis=0)
            mixed = dot(values, weights, 1, 0)
            m_ref[j, :, cols] = largest
            l_ref[j, :, cols] = mixed[SIZE : SIZE + 1, :]
            o_ref[j * SIZE : (j + 1) * SIZE, cols] = mixed[:SIZE, :]

    @pl.when(jnp.logical_not(seen))
    def _():
        m_ref[...] = jnp.full(m_ref.shape, LOW, F32)
        l_ref[...] = jnp.zeros(l_ref.shape, F32)
        o_ref[...] = jnp.zeros(o_ref.shape, F32)


def forward(block, seen, x, wk_t, wv_t, q_t):
    n, d = x.shape
    own = block == 0
    count = 4 if own else 2
    return pl.pallas_call(
        functools.partial(forward_kernel, own, count),
        grid=(HEADS // count,),
        out_shape=(
            jax.ShapeDtypeStruct((HEADS, n, n), BF16),
            jax.ShapeDtypeStruct((HEADS, 1, n), F32),
            jax.ShapeDtypeStruct((HEADS, 1, n), F32),
            jax.ShapeDtypeStruct((d, n), F32),
            jax.ShapeDtypeStruct((d, n), BF16),
            jax.ShapeDtypeStruct((d, n), BF16),
        ),
        in_specs=[SCALAR, whole((n, d)), whole((d, d)), whole((d, d)), head_rows(count, n)],
        out_specs=[
            pl.BlockSpec((count, n, n), lambda h: (h, 0, 0)),
            head_stat(count, n),
            head_stat(count, n),
            head_rows(count, n),
            whole((d, n)),
            whole((d, n)),
        ],
        compiler_params=params(11),
        cost_estimate=cost(4.5 if own else 6),
        name=f"forward_{block}",
    )(seen, x, wk_t, wv_t, q_t)


def join_kernel(count, *refs):
    ms, ls, os = refs[:count], refs[count : 2 * count], refs[2 * count : 3 * count]
    wo_ref, cot_ref, do_ref, att_ref, delta_ref = refs[3 * count : 3 * count + 5]
    cs = refs[3 * count + 5 :]
    do_ref[...] = dot(wo_ref[...], cot_ref[...], 1, 1).astype(BF16)
    for head in range(HEADS):
        rows = slice(head * SIZE, (head + 1) * SIZE)
        largest = functools.reduce(jnp.maximum, [m[head] for m in ms])
        factors = [jnp.exp(m[head] - largest) for m in ms]
        total = functools.reduce(jnp.add, [f * l[head] for f, l in zip(factors, ls)])
        inverse = 1.0 / total
        mixed = None
        for f, o, c in zip(factors, os, cs):
            f = f * inverse
            c[head] = f
            term = o[rows, :] * f
            mixed = term if mixed is None else mixed + term
        attended = mixed.astype(BF16)
        att_ref[rows, :] = attended
        products = attended.astype(F32) * do_ref[rows, :].astype(F32)
        delta_ref[head] = jnp.sum(products, axis=0, keepdims=True)


def join(stats, w_out, cot):
    n, d = cot.shape
    count = len(stats)
    row = jax.ShapeDtypeStruct((HEADS, 1, n), F32)
    return pl.pallas_call(
        functools.partial(join_kernel, count),
        out_shape=(
            jax.ShapeDtypeStruct((d, n), BF16),
            jax.ShapeDtypeStruct((d, n), BF16),
            row,
        )
        + (row,) * count,
        compiler_params=params(),
        cost_estimate=cost(2.5),
        name="join",
    )(*[s[0] for s in stats], *[s[1] for s in stats], *[s[2] for s in stats], w_out, cot)


def backward_kernel(
    own, carried, seen_ref, p_ref, k_ref, v_ref, q_ref, do_ref, c_ref, delta_ref, wk_ref, wv_ref, acc_ref, *rest
):
    carry_refs, rest = rest[:carried], rest[carried:]
    dq_ref, dk_ref, dv_ref, *dx_refs = rest
    step = pl.program_id(0)
    count = p_ref.shape[0]
    seen = seen_ref[0] > 0

    @pl.when(seen)
    def _():
        grads = []
        for j in range(count):
            rows = slice(j * SIZE, (j + 1) * SIZE)
            value_dots = dot(v_ref[rows, :], do_ref[rows, :], 0, 0)
            grads.append(p_ref[j] * (value_dots - delta_ref[j]).astype(BF16))
        for j in range(count):
            rows = slice(j * SIZE, (j + 1) * SIZE)
            out = pl.ds(pl.multiple_of((step * count + j) * SIZE, SIZE), SIZE)
            factor = c_ref[j]
            scaled_q = (q_ref[rows, :].astype(F32) * factor).astype(BF16)
            scaled_do = (do_ref[rows, :].astype(F32) * factor).astype(BF16)
            dq_ref[rows, :] = acc_ref[rows, :] + dot(k_ref[rows, :], grads[j], 1, 0) * factor
            dk_ref[out, :] = dot(scaled_q, grads[j], 1, 1).astype(BF16)
            dv_ref[out, :] = dot(scaled_do, p_ref[j], 1, 1).astype(BF16)

    @pl.when(jnp.logical_not(seen))
    def _():
        out = pl.ds(pl.multiple_of(step * count * SIZE, count * SIZE), count * SIZE)
        dq_ref[...] = acc_ref[...]
        dk_ref[out, :] = jnp.zeros(k_ref.shape, BF16)
        dv_ref[out, :] = jnp.zeros(k_ref.shape, BF16)

    if not own:

        @pl.when(step == HEADS // count - 1)
        def _():
            total = dot(dk_ref[...], wk_ref[...], 0, 0) + dot(dv_ref[...], wv_ref[...], 0, 0)
            for place, carry_ref in enumerate(carry_refs):
                total = total + jnp.where(seen_ref[1 + place] > 0, carry_ref[...], 0).astype(F32)
            dx_refs[0][...] = total.astype(BF16)


def backward(block, seen, p, k, v, q_t, do_t, c, delta, wk_t, wv_t, acc, *carry):
    d, n = q_t.shape
    own = block == 0
    count = 4
    return pl.pallas_call(
        functools.partial(backward_kernel, own, len(carry)),
        grid=(HEADS // count,),
        out_shape=[
            jax.ShapeDtypeStruct((d, n), F32),
            jax.ShapeDtypeStruct((d, n), BF16),
            jax.ShapeDtypeStruct((d, n), BF16),
        ]
        + [jax.ShapeDtypeStruct((n, d), BF16)] * (not own),
        in_specs=[
            SCALAR,
            pl.BlockSpec((count, n, n), lambda h: (h, 0, 0)),
            *[head_rows(count, n)] * 4,
            *[head_stat(count, n)] * 2,
            *[whole((d, d))] * 2,
            head_rows(count, n),
        ]
        + [whole((n, d))] * len(carry),
        out_specs=[head_rows(count, n), whole((d, n)), whole((d, n))] + [whole((n, d))] * (not own),
        compiler_params=params(13),
        cost_estimate=cost(5.5),
        name=f"backward_{block}",
    )(seen, p, k, v, q_t, do_t, c, delta, wk_t, wv_t, acc, *carry)


def final_kernel(flag_ref, att_ref, wo_ref, dq_ref, dk_ref, dv_ref, wq_ref, wk_ref, wv_ref, *refs):
    backs, (out_ref, grad_ref) = refs[:-2], refs[-2:]
    out_ref[...] = dot(att_ref[...], wo_ref[...], 0, 0).astype(BF16)
    total = dot((dq_ref[...] * 0.125).astype(BF16), wq_ref[...], 0, 0)
    total = total + dot(dk_ref[...], wk_ref[...], 0, 0) + dot(dv_ref[...], wv_ref[...], 0, 0)
    for place, back in enumerate(backs):
        total = total + jnp.where(flag_ref[place] > 0, back[...], 0).astype(F32)
    grad_ref[...] = total.astype(BF16)


def finish(flags, att_t, w_out, dq, dk, dv, wq_t, wk_t, wv_t, *backs):
    d, n = att_t.shape
    return pl.pallas_call(
        final_kernel,
        out_shape=(jax.ShapeDtypeStruct((n, d), BF16),) * 2,
        in_specs=[SCALAR] + [pl.BlockSpec(memory_space=pltpu.VMEM)] * (8 + len(backs)),
        compiler_params=params(13),
        cost_estimate=cost(40),
        name="finish",
    )(flags, att_t, w_out, dq, dk, dv, wq_t, wk_t, wv_t, *backs)


def added(parts, xs, total=None):
    for part, x in zip(parts, xs):
        term = dot(part[...], x[...], 1, 0)
        total = term if total is None else total + term
    return total


def early_kernel(count, *refs):
    xs, dks, dvs = refs[:count], refs[count : 2 * count], refs[2 * count : 3 * count]
    att_ref, cot_ref, g_ref = refs[3 * count :]
    g_ref[0] = added(dks, xs)
    g_ref[1] = added(dvs, xs)
    g_ref[2] = dot(cot_ref[...], att_ref[...], 0, 1)


def early_terms(xs, dks, dvs, att_t, cot):
    n, d = cot.shape
    return pl.pallas_call(
        functools.partial(early_kernel, len(xs)),
        out_shape=jax.ShapeDtypeStruct((3, d, d), F32),
        compiler_params=params(14),
        cost_estimate=cost(4),
        name="early_terms",
    )(*xs, *dks, *dvs, att_t, cot)


def weights_kernel(count, core_ref, *refs):
    xs, dks, dvs = refs[:count], refs[count : 2 * count], refs[2 * count : 3 * count]
    dq_ref, early_ref, keep_ref, give_ref, sums = refs[3 * count :]

    def keep(place, value):
        for owner in range(sums.shape[0]):
            sums[owner, 4 * place : 4 * place + 4, :] = value[4 * owner : 4 * owner + 4, :]

    keep(0, dot((dq_ref[...] * 0.125).astype(BF16), xs[0][...], 1, 0))
    keep(1, added(dks, xs, early_ref[0]))
    keep(2, added(dvs, xs, early_ref[1]))
    keep(3, early_ref[2])
    core = core_ref[0]
    for high in range(2):
        here = pl.ds(pl.multiple_of((2 * high + core) * 32, 32), 32)
        there = pl.ds(pl.multiple_of((2 * high + 1 - core) * 32, 32), 32)
        keep_ref[32 * high : 32 * high + 32] = sums[here].astype(BF16)
        give_ref[32 * high : 32 * high + 32] = sums[there].astype(BF16)


def weight_terms(core, xs, dks, dvs, dq, early):
    n, d = xs[0].shape
    half = jax.ShapeDtypeStruct((64, 16, d), BF16)
    return pl.pallas_call(
        functools.partial(weights_kernel, len(xs)),
        out_shape=(half, half),
        in_specs=[SCALAR] + [pl.BlockSpec(memory_space=pltpu.VMEM)] * (3 * len(xs) + 2),
        scratch_shapes=[pltpu.VMEM((128, 16, d), F32)],
        compiler_params=params(18),
        cost_estimate=cost(3.5),
        name="weight_terms",
    )(core, *xs, *dks, *dvs, dq, early)


def either_kernel(flag_ref, first_ref, second_ref, out_ref):
    @pl.when(flag_ref[0] > 0)
    def _():
        out_ref[...] = first_ref[...]

    @pl.when(flag_ref[0] <= 0)
    def _():
        out_ref[...] = second_ref[...]


def either(flag, first, second):
    return pl.pallas_call(
        either_kernel,
        out_shape=jax.ShapeDtypeStruct(first.shape, first.dtype),
        in_specs=[SCALAR] + [pl.BlockSpec(memory_space=pltpu.VMEM)] * 2,
        compiler_params=params(4),
        cost_estimate=cost(0.5),
        name="either",
    )(flag.astype(jnp.int32).reshape(1), first, second)


def sum_kernel(first_ref, second_ref, out_ref):
    out_ref[...] = (first_ref[...].astype(F32) + second_ref[...].astype(F32)).astype(BF16)


def sum_of(first, second):
    return pl.pallas_call(
        sum_kernel,
        out_shape=jax.ShapeDtypeStruct(first.shape, BF16),
        compiler_params=params(6),
        cost_estimate=cost(1),
        name="sum_of",
    )(first, second)


def place(z, x, y):
    return (z % 2) * 16 + (x % 4) * 4 + y % 4


def y_ring(value, step, sources=(0, 1, 2, 3)):
    pairs = [(place(z, x, y), place(z, x, y + step)) for z in range(2) for x in range(4) for y in sources]
    return lax.ppermute(value, "ctx", pairs)


def shifted(value, step):
    return lax.ppermute(
        value, "ctx", [(i, i + step) for i in range(max(0, -step), min(32, 32 - step))]
    )


def body(series, w_query, w_key, w_value, w_out, cotangent):
    x = series[0]
    cot = cotangent[0]
    n, d = x.shape
    position = lax.axis_index("ctx")
    y = position % 4
    x4 = shifted(x, 4)
    x1, x2 = y_ring(x, 1, (0, 1, 2)), y_ring(x, 2, (0, 1))
    q_t, wq_t, wk_t, wv_t = project(x, w_query, w_key, w_value)
    order = (0, 4, 1, 16, 2, 8)
    seen = {p: (position >= p).astype(jnp.int32).reshape(1) for p in order}
    held = {0: forward(0, seen[0], x, wk_t, wv_t, q_t)}
    x4, later, _ = lax.optimization_barrier((x4, x, held[0][1]))
    x1 = either(y == 0, y_ring(x4, 1, (3,)), x1)
    x2 = either(y < 2, y_ring(x4, 2, (2, 3)), x2)
    x16, x8 = shifted(later, 16), shifted(later, 8)
    blocks = {0: x, 1: x1, 2: x2, 4: x4, 8: x8, 16: x16}
    for p in order[1:]:
        held[p] = forward(p, seen[p], blocks[p], wk_t, wv_t, q_t)
    do_t, att_t, delta, *factors = join([held[p][1:4] for p in order], w_out, cot)
    factor = dict(zip(order, factors))
    dq = jnp.zeros((d, n), F32)
    dk, dv = {}, {}
    back = {}
    for p in (1, 2, 8, 16, 0, 4):
        weights, _, _, _, keys, values = held[p]
        flags, carry = seen[p], ()
        if p == 4:
            ready = (1, 2, 8, 16)
            early = early_terms(
                [blocks[i] for i in ready], [dk[i] for i in ready], [dv[i] for i in ready], att_t, cot
            )
            early, back[1], back[2] = lax.optimization_barrier((early, back[1], back[2]))
            wraps = jnp.stack([y == 3, y >= 2]).astype(jnp.int32)
            flags, carry = jnp.concatenate([flags, wraps]), (back[1], back[2])
        dq, dk[p], dv[p], *sent = backward(
            p, flags, weights, keys, values, q_t, do_t, factor[p], delta, wk_t, wv_t, dq, *carry
        )
        if p in (1, 2):
            back[p] = y_ring(sent[0], -p)
        elif p:
            back[p] = shifted(sent[0], -p)
    core = lax.axis_index("dp") % 2
    kept, given = weight_terms(
        core.astype(jnp.int32).reshape(1), [x, x4], [dk[0], dk[4]], [dv[0], dv[4]], dq, early
    )
    kept, given, back[8], back[16] = lax.optimization_barrier((kept, given, back[8], back[16]))
    given = lax.ppermute(given, "dp", [(0, 1), (1, 0), (2, 3), (3, 2)])
    terms = sum_of(kept, given)
    same_core = [[32 * i + j for i in (k, k + 2) for j in range(32)] for k in range(2)]
    terms = lax.all_to_all(terms, ("dp", "ctx"), 0, 0, axis_index_groups=same_core, tiled=True)
    grads = jnp.sum(terms.astype(F32), axis=0).reshape(4, 4, d).transpose(0, 2, 1)
    flags = jnp.stack([y >= 0, y >= 0, y >= 0, y < 3, y < 2]).astype(jnp.int32)
    output, input_grad = finish(
        flags, att_t, w_out, dq, dk[0], dv[0], wq_t, wk_t, wv_t, back[4], back[8], back[16], back[1], back[2]
    )
    return (output[None], input_grad[None], grads[0], grads[1], grads[2], grads[3])


def solution(mesh):
    return jax.shard_map(
        body,
        mesh=mesh,
        in_specs=(P("dp", "ctx", None), P(), P(), P(), P(), P("dp", "ctx", None)),
        out_specs=(
            P("dp", "ctx", None),
            P("dp", "ctx", None),
            P(None, ("dp", "ctx")),
            P(None, ("dp", "ctx")),
            P(None, ("dp", "ctx")),
            P(None, ("dp", "ctx")),
        ),
        check_vma=False,
    )
```

```python
import functools

import jax
import jax.numpy as jnp
from jax import lax
from jax.experimental import pallas as pl
from jax.experimental.pallas import tpu as pltpu
from jax.sharding import PartitionSpec as P

HEADS = 8
SIZE = 64
F32 = jnp.float32
BF16 = jnp.bfloat16
LOW = -3.0e38
MIB = 2**20


def dot(left, right, left_dim, right_dim):
    return lax.dot_general(
        left, right, (((left_dim,), (right_dim,)), ((), ())), preferred_element_type=F32
    )


def whole(shape):
    return pl.BlockSpec(shape, lambda *_: (0,) * len(shape), pipeline_mode=pl.Buffered(1))


def head_rows(count, width):
    return pl.BlockSpec((count * SIZE, width), lambda h: (h, 0))


def head_stat(count, width):
    return pl.BlockSpec((count, 1, width), lambda h: (h, 0, 0))


SCALAR = pl.BlockSpec(memory_space=pltpu.SMEM)


def params(mib=16):
    return pltpu.CompilerParams(vmem_limit_bytes=mib * MIB)


def cost(microseconds):
    return pl.CostEstimate(flops=int(microseconds * 1.1e9), bytes_accessed=MIB, transcendentals=0)


def project_kernel(x_ref, wq_ref, wk_ref, wv_ref, q_ref, wq_t_ref, wk_t_ref, wv_t_ref):
    wq_t_ref[...] = wq_ref[...].T
    q_ref[...] = dot(wq_t_ref[...], x_ref[...], 1, 1).astype(BF16) * jnp.asarray(0.125, BF16)
    wk_t_ref[...] = wk_ref[...].T
    wv_t_ref[...] = wv_ref[...].T


def project(x, w_query, w_key, w_value):
    n, d = x.shape
    square = jax.ShapeDtypeStruct((d, d), BF16)
    return pl.pallas_call(
        project_kernel,
        out_shape=(jax.ShapeDtypeStruct((d, n), BF16),) + (square,) * 3,
        compiler_params=params(12),
        cost_estimate=cost(2),
        name="project",
    )(x, w_query, w_key, w_value)


def forward_kernel(own, count, seen_ref, x_ref, wk_ref, wv_ref, q_ref, p_ref, m_ref, l_ref, o_ref, k_ref, v_ref):
    step = pl.program_id(0)
    seen = seen_ref[0] > 0

    @pl.when(jnp.logical_and(seen, step == 0))
    def _():
        k_ref[...] = dot(wk_ref[...], x_ref[...], 1, 1).astype(BF16)
        v_ref[...] = dot(wv_ref[...], x_ref[...], 1, 1).astype(BF16)

    @pl.when(seen)
    def _():
        n = q_ref.shape[1]
        chunk = n // 2 if own else n
        parts = [(j, start) for j in range(count) for start in range(0, n, chunk)]
        scores = []
        for j, start in parts:
            known = start + chunk if own else n
            keys = k_ref[pl.ds(pl.multiple_of((step * count + j) * SIZE, SIZE), SIZE), :known]
            scores.append(dot(keys, q_ref[j * SIZE : (j + 1) * SIZE, start : start + chunk], 0, 0))
        for (j, start), score in zip(parts, scores):
            known = start + chunk if own else n
            cols = slice(start, start + chunk)
            if own:
                at_key = lax.broadcasted_iota(jnp.int32, score.shape, 0)
                at_query = lax.broadcasted_iota(jnp.int32, score.shape, 1) + start
                score = jnp.where(at_key <= at_query, score, LOW)
            largest = jnp.max(score, axis=0, keepdims=True)
            weights = jnp.exp(score - largest).astype(BF16)
            p_ref[j, :known, cols] = weights
            if known < n:
                p_ref[j, known:, cols] = jnp.zeros((n - known, chunk), BF16)
            values = v_ref[pl.ds(pl.multiple_of((step * count + j) * SIZE, SIZE), SIZE), :known]
            values = jnp.concatenate([values, jnp.ones((16, known), BF16)], axis=0)
            mixed = dot(values, weights, 1, 0)
            m_ref[j, :, cols] = largest
            l_ref[j, :, cols] = mixed[SIZE : SIZE + 1, :]
            o_ref[j * SIZE : (j + 1) * SIZE, cols] = mixed[:SIZE, :]

    @pl.when(jnp.logical_not(seen))
    def _():
        m_ref[...] = jnp.full(m_ref.shape, LOW, F32)
        l_ref[...] = jnp.zeros(l_ref.shape, F32)
        o_ref[...] = jnp.zeros(o_ref.shape, F32)


def forward(block, seen, x, wk_t, wv_t, q_t):
    n, d = x.shape
    own = block == 0
    count = 4 if own else 2
    return pl.pallas_call(
        functools.partial(forward_kernel, own, count),
        grid=(HEADS // count,),
        out_shape=(
            jax.ShapeDtypeStruct((HEADS, n, n), BF16),
            jax.ShapeDtypeStruct((HEADS, 1, n), F32),
            jax.ShapeDtypeStruct((HEADS, 1, n), F32),
            jax.ShapeDtypeStruct((d, n), F32),
            jax.ShapeDtypeStruct((d, n), BF16),
            jax.ShapeDtypeStruct((d, n), BF16),
        ),
        in_specs=[SCALAR, whole((n, d)), whole((d, d)), whole((d, d)), head_rows(count, n)],
        out_specs=[
            pl.BlockSpec((count, n, n), lambda h: (h, 0, 0)),
            head_stat(count, n),
            head_stat(count, n),
            head_rows(count, n),
            whole((d, n)),
            whole((d, n)),
        ],
        compiler_params=params(11),
        cost_estimate=cost(4.5 if own else 6),
        name=f"forward_{block}",
    )(seen, x, wk_t, wv_t, q_t)


def join_kernel(count, *refs):
    ms, ls, os = refs[:count], refs[count : 2 * count], refs[2 * count : 3 * count]
    wo_ref, cot_ref, do_ref, att_ref, delta_ref = refs[3 * count : 3 * count + 5]
    cs = refs[3 * count + 5 :]
    do_ref[...] = dot(wo_ref[...], cot_ref[...], 1, 1).astype(BF16)
    for head in range(HEADS):
        rows = slice(head * SIZE, (head + 1) * SIZE)
        largest = functools.reduce(jnp.maximum, [m[head] for m in ms])
        factors = [jnp.exp(m[head] - largest) for m in ms]
        total = functools.reduce(jnp.add, [f * l[head] for f, l in zip(factors, ls)])
        inverse = 1.0 / total
        mixed = None
        for f, o, c in zip(factors, os, cs):
            f = f * inverse
            c[head] = f
            term = o[rows, :] * f
            mixed = term if mixed is None else mixed + term
        attended = mixed.astype(BF16)
        att_ref[rows, :] = attended
        products = attended.astype(F32) * do_ref[rows, :].astype(F32)
        delta_ref[head] = jnp.sum(products, axis=0, keepdims=True)


def join(stats, w_out, cot):
    n, d = cot.shape
    count = len(stats)
    row = jax.ShapeDtypeStruct((HEADS, 1, n), F32)
    return pl.pallas_call(
        functools.partial(join_kernel, count),
        out_shape=(
            jax.ShapeDtypeStruct((d, n), BF16),
            jax.ShapeDtypeStruct((d, n), BF16),
            row,
        )
        + (row,) * count,
        compiler_params=params(),
        cost_estimate=cost(2.5),
        name="join",
    )(*[s[0] for s in stats], *[s[1] for s in stats], *[s[2] for s in stats], w_out, cot)


def backward_kernel(
    sends, seen_ref, p_ref, k_ref, v_ref, q_ref, do_ref, c_ref, delta_ref, wk_ref, wv_ref, acc_ref,
    dq_ref, dk_ref, dv_ref, *dx_refs,
):
    step = pl.program_id(0)
    count = p_ref.shape[0]
    seen = seen_ref[0] > 0

    @pl.when(seen)
    def _():
        grads = []
        for j in range(count):
            rows = slice(j * SIZE, (j + 1) * SIZE)
            value_dots = dot(v_ref[rows, :], do_ref[rows, :], 0, 0)
            grads.append(p_ref[j] * (value_dots - delta_ref[j]).astype(BF16))
        for j in range(count):
            rows = slice(j * SIZE, (j + 1) * SIZE)
            out = pl.ds(pl.multiple_of((step * count + j) * SIZE, SIZE), SIZE)
            factor = c_ref[j]
            scaled_q = (q_ref[rows, :].astype(F32) * factor).astype(BF16)
            scaled_do = (do_ref[rows, :].astype(F32) * factor).astype(BF16)
            dq_ref[rows, :] = acc_ref[rows, :] + dot(k_ref[rows, :], grads[j], 1, 0) * factor
            dk_ref[out, :] = dot(scaled_q, grads[j], 1, 1).astype(BF16)
            dv_ref[out, :] = dot(scaled_do, p_ref[j], 1, 1).astype(BF16)

    @pl.when(jnp.logical_not(seen))
    def _():
        out = pl.ds(pl.multiple_of(step * count * SIZE, count * SIZE), count * SIZE)
        dq_ref[...] = acc_ref[...]
        dk_ref[out, :] = jnp.zeros(k_ref.shape, BF16)
        dv_ref[out, :] = jnp.zeros(k_ref.shape, BF16)

    if sends:

        @pl.when(step == HEADS // count - 1)
        def _():
            total = dot(dk_ref[...], wk_ref[...], 0, 0) + dot(dv_ref[...], wv_ref[...], 0, 0)
            dx_refs[0][...] = total.astype(BF16)


def backward(block, seen, p, k, v, q_t, do_t, c, delta, wk_t, wv_t, acc):
    d, n = q_t.shape
    sends = block not in (0, 4)
    count = 4
    return pl.pallas_call(
        functools.partial(backward_kernel, sends),
        grid=(HEADS // count,),
        out_shape=[
            jax.ShapeDtypeStruct((d, n), F32),
            jax.ShapeDtypeStruct((d, n), BF16),
            jax.ShapeDtypeStruct((d, n), BF16),
        ]
        + [jax.ShapeDtypeStruct((n, d), BF16)] * sends,
        in_specs=[
            SCALAR,
            pl.BlockSpec((count, n, n), lambda h: (h, 0, 0)),
            *[head_rows(count, n)] * 4,
            *[head_stat(count, n)] * 2,
            *[whole((d, d))] * 2,
            head_rows(count, n),
        ],
        out_specs=[head_rows(count, n), whole((d, n)), whole((d, n))] + [whole((n, d))] * sends,
        compiler_params=params(13),
        cost_estimate=cost(5.5),
        name=f"backward_{block}",
    )(seen, p, k, v, q_t, do_t, c, delta, wk_t, wv_t, acc)


def returned_kernel(flag_ref, dk_ref, dv_ref, wk_ref, wv_ref, *refs):
    one, two, eight, sixteen, sent_ref, sum_ref = refs
    total = dot(dk_ref[...], wk_ref[...], 0, 0) + dot(dv_ref[...], wv_ref[...], 0, 0)
    total = total + jnp.where(flag_ref[0] > 0, one[...], 0).astype(F32)
    total = total + jnp.where(flag_ref[1] > 0, two[...], 0).astype(F32)
    sent_ref[...] = total.astype(BF16)
    kept = eight[...].astype(F32) + sixteen[...].astype(F32)
    kept = kept + jnp.where(flag_ref[0] > 0, 0, one[...]).astype(F32)
    sum_ref[...] = kept + jnp.where(flag_ref[1] > 0, 0, two[...]).astype(F32)


def returned(flags, dk, dv, wk_t, wv_t, *backs):
    d, n = dk.shape
    return pl.pallas_call(
        returned_kernel,
        out_shape=(jax.ShapeDtypeStruct((n, d), BF16), jax.ShapeDtypeStruct((n, d), F32)),
        in_specs=[SCALAR] + [pl.BlockSpec(memory_space=pltpu.VMEM)] * 8,
        compiler_params=params(10),
        cost_estimate=cost(20),
        name="returned",
    )(flags, dk, dv, wk_t, wv_t, *backs)


def final_kernel(att_ref, wo_ref, dq_ref, dk_ref, dv_ref, wq_ref, wk_ref, wv_ref, sum_ref, four, out_ref, grad_ref):
    out_ref[...] = dot(att_ref[...], wo_ref[...], 0, 0).astype(BF16)
    total = dot((dq_ref[...] * 0.125).astype(BF16), wq_ref[...], 0, 0)
    total = total + dot(dk_ref[...], wk_ref[...], 0, 0) + dot(dv_ref[...], wv_ref[...], 0, 0)
    grad_ref[...] = (total + sum_ref[...] + four[...].astype(F32)).astype(BF16)


def finish(att_t, w_out, dq, dk, dv, wq_t, wk_t, wv_t, total, four):
    d, n = att_t.shape
    return pl.pallas_call(
        final_kernel,
        out_shape=(jax.ShapeDtypeStruct((n, d), BF16),) * 2,
        compiler_params=params(13),
        cost_estimate=cost(40),
        name="finish",
    )(att_t, w_out, dq, dk, dv, wq_t, wk_t, wv_t, total, four)


def added(parts, xs, total=None):
    for part, x in zip(parts, xs):
        term = dot(part[...], x[...], 1, 0)
        total = term if total is None else total + term
    return total


def early_kernel(count, *refs):
    xs, dks, dvs = refs[:count], refs[count : 2 * count], refs[2 * count : 3 * count]
    att_ref, cot_ref, g_ref = refs[3 * count :]
    g_ref[0] = added(dks, xs)
    g_ref[1] = added(dvs, xs)
    g_ref[2] = dot(cot_ref[...], att_ref[...], 0, 1)


def early_terms(xs, dks, dvs, att_t, cot):
    n, d = cot.shape
    return pl.pallas_call(
        functools.partial(early_kernel, len(xs)),
        out_shape=jax.ShapeDtypeStruct((3, d, d), F32),
        compiler_params=params(14),
        cost_estimate=cost(4),
        name="early_terms",
    )(*xs, *dks, *dvs, att_t, cot)


def weights_kernel(count, core_ref, *refs):
    xs, dks, dvs = refs[:count], refs[count : 2 * count], refs[2 * count : 3 * count]
    dq_ref, early_ref, keep_ref, give_ref, sums = refs[3 * count :]

    def keep(place, value):
        for owner in range(sums.shape[0]):
            sums[owner, 4 * place : 4 * place + 4, :] = value[4 * owner : 4 * owner + 4, :]

    keep(0, dot((dq_ref[...] * 0.125).astype(BF16), xs[0][...], 1, 0))
    keep(1, added(dks, xs, early_ref[0]))
    keep(2, added(dvs, xs, early_ref[1]))
    keep(3, early_ref[2])
    core = core_ref[0]
    for high in range(2):
        here = pl.ds(pl.multiple_of((2 * high + core) * 32, 32), 32)
        there = pl.ds(pl.multiple_of((2 * high + 1 - core) * 32, 32), 32)
        keep_ref[32 * high : 32 * high + 32] = sums[here].astype(BF16)
        give_ref[32 * high : 32 * high + 32] = sums[there].astype(BF16)


def weight_terms(core, xs, dks, dvs, dq, early):
    n, d = xs[0].shape
    half = jax.ShapeDtypeStruct((64, 16, d), BF16)
    return pl.pallas_call(
        functools.partial(weights_kernel, len(xs)),
        out_shape=(half, half),
        in_specs=[SCALAR] + [pl.BlockSpec(memory_space=pltpu.VMEM)] * (3 * len(xs) + 2),
        scratch_shapes=[pltpu.VMEM((128, 16, d), F32)],
        compiler_params=params(18),
        cost_estimate=cost(3.5),
        name="weight_terms",
    )(core, *xs, *dks, *dvs, dq, early)


def either_kernel(flag_ref, first_ref, second_ref, out_ref):
    @pl.when(flag_ref[0] > 0)
    def _():
        out_ref[...] = first_ref[...]

    @pl.when(flag_ref[0] <= 0)
    def _():
        out_ref[...] = second_ref[...]


def either(flag, first, second):
    return pl.pallas_call(
        either_kernel,
        out_shape=jax.ShapeDtypeStruct(first.shape, first.dtype),
        in_specs=[SCALAR] + [pl.BlockSpec(memory_space=pltpu.VMEM)] * 2,
        compiler_params=params(4),
        cost_estimate=cost(0.5),
        name="either",
    )(flag.astype(jnp.int32).reshape(1), first, second)


def sum_kernel(first_ref, second_ref, out_ref):
    out_ref[...] = (first_ref[...].astype(F32) + second_ref[...].astype(F32)).astype(BF16)


def sum_of(first, second):
    return pl.pallas_call(
        sum_kernel,
        out_shape=jax.ShapeDtypeStruct(first.shape, BF16),
        compiler_params=params(6),
        cost_estimate=cost(1),
        name="sum_of",
    )(first, second)


def place(z, x, y):
    return (z % 2) * 16 + (x % 4) * 4 + y % 4


def y_ring(value, step, sources=(0, 1, 2, 3)):
    pairs = [(place(z, x, y), place(z, x, y + step)) for z in range(2) for x in range(4) for y in sources]
    return lax.ppermute(value, "ctx", pairs)


def shifted(value, step):
    return lax.ppermute(
        value, "ctx", [(i, i + step) for i in range(max(0, -step), min(32, 32 - step))]
    )


def body(series, w_query, w_key, w_value, w_out, cotangent):
    x = series[0]
    cot = cotangent[0]
    n, d = x.shape
    position = lax.axis_index("ctx")
    y = position % 4
    x4 = shifted(x, 4)
    x1, x2 = shifted(x, 1), y_ring(x, 2, (0, 1))
    q_t, wq_t, wk_t, wv_t = project(x, w_query, w_key, w_value)
    order = (0, 4, 1, 16, 2, 8)
    seen = {p: (position >= p).astype(jnp.int32).reshape(1) for p in order}
    held = {0: forward(0, seen[0], x, wk_t, wv_t, q_t)}
    x4, later, _ = lax.optimization_barrier((x4, x, held[0][1]))
    x2 = either(y < 2, y_ring(x4, 2, (2, 3)), x2)
    held[4] = forward(4, seen[4], x4, wk_t, wv_t, q_t)
    latest, _ = lax.optimization_barrier((later, held[4][1]))
    x16, x8 = shifted(later, 16), shifted(latest, 8)
    blocks = {0: x, 1: x1, 2: x2, 4: x4, 8: x8, 16: x16}
    for p in order[2:]:
        held[p] = forward(p, seen[p], blocks[p], wk_t, wv_t, q_t)
    do_t, att_t, delta, *factors = join([held[p][1:4] for p in order], w_out, cot)
    factor = dict(zip(order, factors))
    dq = jnp.zeros((d, n), F32)
    dk, dv = {}, {}
    back = {}
    for p in (1, 2, 8, 16, 0, 4):
        weights, _, _, _, keys, values = held[p]
        dq, dk[p], dv[p], *sent = backward(
            p, seen[p], weights, keys, values, q_t, do_t, factor[p], delta, wk_t, wv_t, dq
        )
        if p in (1, 2):
            back[p] = y_ring(sent[0], -p)
        elif sent:
            back[p] = shifted(sent[0], -p)
    dk[1], back[1], back[2] = lax.optimization_barrier((dk[1], back[1], back[2]))
    ready = (1, 2, 8, 16)
    early = early_terms([blocks[i] for i in ready], [dk[i] for i in ready], [dv[i] for i in ready], att_t, cot)
    core = lax.axis_index("dp") % 2
    kept, given = weight_terms(
        core.astype(jnp.int32).reshape(1), [x, x4], [dk[0], dk[4]], [dv[0], dv[4]], dq, early
    )
    wraps = jnp.stack([y == 3, y >= 2]).astype(jnp.int32)
    sent, total = returned(wraps, dk[4], dv[4], wk_t, wv_t, back[1], back[2], back[8], back[16])
    back[4] = shifted(sent, -4)
    given = lax.ppermute(given, "dp", [(0, 1), (1, 0), (2, 3), (3, 2)])
    terms = sum_of(kept, given)
    same_core = [[32 * i + j for i in (k, k + 2) for j in range(32)] for k in range(2)]
    terms = lax.all_to_all(terms, ("dp", "ctx"), 0, 0, axis_index_groups=same_core, tiled=True)
    grads = jnp.sum(terms.astype(F32), axis=0).reshape(4, 4, d).transpose(0, 2, 1)
    output, input_grad = finish(att_t, w_out, dq, dk[0], dv[0], wq_t, wk_t, wv_t, total, back[4])
    return (output[None], input_grad[None], grads[0], grads[1], grads[2], grads[3])


def solution(mesh):
    return jax.shard_map(
        body,
        mesh=mesh,
        in_specs=(P("dp", "ctx", None), P(), P(), P(), P(), P("dp", "ctx", None)),
        out_specs=(
            P("dp", "ctx", None),
            P("dp", "ctx", None),
            P(None, ("dp", "ctx")),
            P(None, ("dp", "ctx")),
            P(None, ("dp", "ctx")),
            P(None, ("dp", "ctx")),
        ),
        check_vma=False,
    )
```

```python
import functools

import jax
import jax.numpy as jnp
from jax import lax
from jax.experimental import pallas as pl
from jax.experimental.pallas import tpu as pltpu
from jax.sharding import PartitionSpec as P

HEADS = 8
SIZE = 64
F32 = jnp.float32
BF16 = jnp.bfloat16
LOW = -3.0e38
MIB = 2**20


def dot(left, right, left_dim, right_dim):
    return lax.dot_general(
        left, right, (((left_dim,), (right_dim,)), ((), ())), preferred_element_type=F32
    )


def whole(shape):
    return pl.BlockSpec(shape, lambda *_: (0,) * len(shape), pipeline_mode=pl.Buffered(1))


def head_rows(count, width):
    return pl.BlockSpec((count * SIZE, width), lambda h: (h, 0))


def head_stat(count, width):
    return pl.BlockSpec((count, 1, width), lambda h: (h, 0, 0))


SCALAR = pl.BlockSpec(memory_space=pltpu.SMEM)


def params(mib=16):
    return pltpu.CompilerParams(vmem_limit_bytes=mib * MIB)


def cost(microseconds):
    return pl.CostEstimate(flops=int(microseconds * 1.1e9), bytes_accessed=MIB, transcendentals=0)


def project_kernel(x_ref, wq_ref, wk_ref, wv_ref, q_ref, wq_t_ref, wk_t_ref, wv_t_ref):
    wq_t_ref[...] = wq_ref[...].T
    q_ref[...] = dot(wq_t_ref[...], x_ref[...], 1, 1).astype(BF16) * jnp.asarray(0.125, BF16)
    wk_t_ref[...] = wk_ref[...].T
    wv_t_ref[...] = wv_ref[...].T


def project(x, w_query, w_key, w_value):
    n, d = x.shape
    square = jax.ShapeDtypeStruct((d, d), BF16)
    return pl.pallas_call(
        project_kernel,
        out_shape=(jax.ShapeDtypeStruct((d, n), BF16),) + (square,) * 3,
        compiler_params=params(12),
        cost_estimate=cost(2),
        name="project",
    )(x, w_query, w_key, w_value)


def forward_kernel(own, count, seen_ref, x_ref, wk_ref, wv_ref, q_ref, p_ref, m_ref, l_ref, o_ref, k_ref, v_ref):
    step = pl.program_id(0)
    seen = seen_ref[0] > 0

    @pl.when(jnp.logical_and(seen, step == 0))
    def _():
        k_ref[...] = dot(wk_ref[...], x_ref[...], 1, 1).astype(BF16)
        v_ref[...] = dot(wv_ref[...], x_ref[...], 1, 1).astype(BF16)

    @pl.when(seen)
    def _():
        n = q_ref.shape[1]
        chunk = n // 2 if own else n
        parts = [(j, start) for j in range(count) for start in range(0, n, chunk)]
        scores = []
        for j, start in parts:
            known = start + chunk if own else n
            keys = k_ref[pl.ds(pl.multiple_of((step * count + j) * SIZE, SIZE), SIZE), :known]
            scores.append(dot(keys, q_ref[j * SIZE : (j + 1) * SIZE, start : start + chunk], 0, 0))
        for (j, start), score in zip(parts, scores):
            known = start + chunk if own else n
            cols = slice(start, start + chunk)
            if own:
                at_key = lax.broadcasted_iota(jnp.int32, score.shape, 0)
                at_query = lax.broadcasted_iota(jnp.int32, score.shape, 1) + start
                score = jnp.where(at_key <= at_query, score, LOW)
            largest = jnp.max(score, axis=0, keepdims=True)
            weights = jnp.exp(score - largest).astype(BF16)
            p_ref[j, :known, cols] = weights
            if known < n:
                p_ref[j, known:, cols] = jnp.zeros((n - known, chunk), BF16)
            values = v_ref[pl.ds(pl.multiple_of((step * count + j) * SIZE, SIZE), SIZE), :known]
            values = jnp.concatenate([values, jnp.ones((16, known), BF16)], axis=0)
            mixed = dot(values, weights, 1, 0)
            m_ref[j, :, cols] = largest
            l_ref[j, :, cols] = mixed[SIZE : SIZE + 1, :]
            o_ref[j * SIZE : (j + 1) * SIZE, cols] = mixed[:SIZE, :]

    @pl.when(jnp.logical_not(seen))
    def _():
        m_ref[...] = jnp.full(m_ref.shape, LOW, F32)
        l_ref[...] = jnp.zeros(l_ref.shape, F32)
        o_ref[...] = jnp.zeros(o_ref.shape, F32)


def forward(block, seen, x, wk_t, wv_t, q_t):
    n, d = x.shape
    own = block == 0
    count = 4 if own else 2
    return pl.pallas_call(
        functools.partial(forward_kernel, own, count),
        grid=(HEADS // count,),
        out_shape=(
            jax.ShapeDtypeStruct((HEADS, n, n), BF16),
            jax.ShapeDtypeStruct((HEADS, 1, n), F32),
            jax.ShapeDtypeStruct((HEADS, 1, n), F32),
            jax.ShapeDtypeStruct((d, n), F32),
            jax.ShapeDtypeStruct((d, n), BF16),
            jax.ShapeDtypeStruct((d, n), BF16),
        ),
        in_specs=[SCALAR, whole((n, d)), whole((d, d)), whole((d, d)), head_rows(count, n)],
        out_specs=[
            pl.BlockSpec((count, n, n), lambda h: (h, 0, 0)),
            head_stat(count, n),
            head_stat(count, n),
            head_rows(count, n),
            whole((d, n)),
            whole((d, n)),
        ],
        compiler_params=params(11),
        cost_estimate=cost(4.5 if own else 6),
        name=f"forward_{block}",
    )(seen, x, wk_t, wv_t, q_t)


def join_kernel(count, *refs):
    ms, ls, os = refs[:count], refs[count : 2 * count], refs[2 * count : 3 * count]
    wo_ref, cot_ref, do_ref, att_ref, delta_ref = refs[3 * count : 3 * count + 5]
    cs = refs[3 * count + 5 :]
    do_ref[...] = dot(wo_ref[...], cot_ref[...], 1, 1).astype(BF16)
    for head in range(HEADS):
        rows = slice(head * SIZE, (head + 1) * SIZE)
        largest = functools.reduce(jnp.maximum, [m[head] for m in ms])
        factors = [jnp.exp(m[head] - largest) for m in ms]
        total = functools.reduce(jnp.add, [f * l[head] for f, l in zip(factors, ls)])
        inverse = 1.0 / total
        mixed = None
        for f, o, c in zip(factors, os, cs):
            f = f * inverse
            c[head] = f
            term = o[rows, :] * f
            mixed = term if mixed is None else mixed + term
        attended = mixed.astype(BF16)
        att_ref[rows, :] = attended
        products = attended.astype(F32) * do_ref[rows, :].astype(F32)
        delta_ref[head] = jnp.sum(products, axis=0, keepdims=True)


def join(stats, w_out, cot):
    n, d = cot.shape
    count = len(stats)
    row = jax.ShapeDtypeStruct((HEADS, 1, n), F32)
    return pl.pallas_call(
        functools.partial(join_kernel, count),
        out_shape=(
            jax.ShapeDtypeStruct((d, n), BF16),
            jax.ShapeDtypeStruct((d, n), BF16),
            row,
        )
        + (row,) * count,
        compiler_params=params(),
        cost_estimate=cost(2.5),
        name="join",
    )(*[s[0] for s in stats], *[s[1] for s in stats], *[s[2] for s in stats], w_out, cot)


def backward_kernel(
    own, sends, seen_ref, p_ref, k_ref, v_ref, q_ref, do_ref, c_ref, delta_ref, wk_ref, wv_ref, acc_ref,
    dq_ref, dk_ref, dv_ref, *dx_refs,
):
    step = pl.program_id(0)
    count = p_ref.shape[0]
    seen = seen_ref[0] > 0

    def far_block():
        grads = []
        for j in range(count):
            rows = slice(j * SIZE, (j + 1) * SIZE)
            value_dots = dot(v_ref[rows, :], do_ref[rows, :], 0, 0)
            grads.append(p_ref[j] * (value_dots - delta_ref[j]).astype(BF16))
        for j in range(count):
            rows = slice(j * SIZE, (j + 1) * SIZE)
            out = pl.ds(pl.multiple_of((step * count + j) * SIZE, SIZE), SIZE)
            factor = c_ref[j]
            scaled_q = (q_ref[rows, :].astype(F32) * factor).astype(BF16)
            scaled_do = (do_ref[rows, :].astype(F32) * factor).astype(BF16)
            dq_ref[rows, :] = acc_ref[rows, :] + dot(k_ref[rows, :], grads[j], 1, 0) * factor
            dk_ref[out, :] = dot(scaled_q, grads[j], 1, 1).astype(BF16)
            dv_ref[out, :] = dot(scaled_do, p_ref[j], 1, 1).astype(BF16)

    def own_block():
        n = q_ref.shape[1]
        half = n // 2
        parts = ((0, half, half), (half, n, n))
        grads = []
        for j in range(count):
            rows = slice(j * SIZE, (j + 1) * SIZE)
            for start, stop, known in parts:
                value_dots = dot(v_ref[rows, :known], do_ref[rows, start:stop], 0, 0)
                delta = delta_ref[j, :, start:stop]
                grads.append(p_ref[j, :known, start:stop] * (value_dots - delta).astype(BF16))
        for j in range(count):
            rows = slice(j * SIZE, (j + 1) * SIZE)
            out = pl.ds(pl.multiple_of((step * count + j) * SIZE, SIZE), SIZE)
            dks, dvs = [], []
            for (start, stop, known), grad in zip(parts, grads[2 * j : 2 * j + 2]):
                factor = c_ref[j, :, start:stop]
                scaled_q = (q_ref[rows, start:stop].astype(F32) * factor).astype(BF16)
                scaled_do = (do_ref[rows, start:stop].astype(F32) * factor).astype(BF16)
                dq = dot(k_ref[rows, :known], grad, 1, 0) * factor
                dq_ref[rows, start:stop] = acc_ref[rows, start:stop] + dq
                dks.append(dot(scaled_q, grad, 1, 1))
                dvs.append(dot(scaled_do, p_ref[j, :known, start:stop], 1, 1))
            for ref, (first, second) in ((dk_ref, dks), (dv_ref, dvs)):
                ref[out, :half] = (first + second[:, :half]).astype(BF16)
                ref[out, half:] = second[:, half:].astype(BF16)

    pl.when(seen)(own_block if own else far_block)

    @pl.when(jnp.logical_not(seen))
    def _():
        out = pl.ds(pl.multiple_of(step * count * SIZE, count * SIZE), count * SIZE)
        dq_ref[...] = acc_ref[...]
        dk_ref[out, :] = jnp.zeros(k_ref.shape, BF16)
        dv_ref[out, :] = jnp.zeros(k_ref.shape, BF16)

    if sends:

        @pl.when(step == HEADS // count - 1)
        def _():
            total = dot(dk_ref[...], wk_ref[...], 0, 0) + dot(dv_ref[...], wv_ref[...], 0, 0)
            dx_refs[0][...] = total.astype(BF16)


def backward(block, seen, p, k, v, q_t, do_t, c, delta, wk_t, wv_t, acc):
    d, n = q_t.shape
    sends = block not in (0, 4)
    count = 4
    return pl.pallas_call(
        functools.partial(backward_kernel, block == 0, sends),
        grid=(HEADS // count,),
        out_shape=[
            jax.ShapeDtypeStruct((d, n), F32),
            jax.ShapeDtypeStruct((d, n), BF16),
            jax.ShapeDtypeStruct((d, n), BF16),
        ]
        + [jax.ShapeDtypeStruct((n, d), BF16)] * sends,
        in_specs=[
            SCALAR,
            pl.BlockSpec((count, n, n), lambda h: (h, 0, 0)),
            *[head_rows(count, n)] * 4,
            *[head_stat(count, n)] * 2,
            *[whole((d, d))] * 2,
            head_rows(count, n),
        ],
        out_specs=[head_rows(count, n), whole((d, n)), whole((d, n))] + [whole((n, d))] * sends,
        compiler_params=params(13),
        cost_estimate=cost(5.5),
        name=f"backward_{block}",
    )(seen, p, k, v, q_t, do_t, c, delta, wk_t, wv_t, acc)


def returned_kernel(flag_ref, dk_ref, dv_ref, wk_ref, wv_ref, *refs):
    one, two, eight, sixteen, sent_ref, sum_ref = refs
    total = dot(dk_ref[...], wk_ref[...], 0, 0) + dot(dv_ref[...], wv_ref[...], 0, 0)
    total = total + jnp.where(flag_ref[0] > 0, one[...], 0).astype(F32)
    total = total + jnp.where(flag_ref[1] > 0, two[...], 0).astype(F32)
    sent_ref[...] = total.astype(BF16)
    kept = eight[...].astype(F32) + sixteen[...].astype(F32)
    kept = kept + jnp.where(flag_ref[0] > 0, 0, one[...]).astype(F32)
    sum_ref[...] = kept + jnp.where(flag_ref[1] > 0, 0, two[...]).astype(F32)


def returned(flags, dk, dv, wk_t, wv_t, *backs):
    d, n = dk.shape
    return pl.pallas_call(
        returned_kernel,
        out_shape=(jax.ShapeDtypeStruct((n, d), BF16), jax.ShapeDtypeStruct((n, d), F32)),
        in_specs=[SCALAR] + [pl.BlockSpec(memory_space=pltpu.VMEM)] * 8,
        compiler_params=params(10),
        cost_estimate=cost(20),
        name="returned",
    )(flags, dk, dv, wk_t, wv_t, *backs)


def final_kernel(att_ref, wo_ref, dq_ref, dk_ref, dv_ref, wq_ref, wk_ref, wv_ref, sum_ref, four, out_ref, grad_ref):
    out_ref[...] = dot(att_ref[...], wo_ref[...], 0, 0).astype(BF16)
    total = dot((dq_ref[...] * 0.125).astype(BF16), wq_ref[...], 0, 0)
    total = total + dot(dk_ref[...], wk_ref[...], 0, 0) + dot(dv_ref[...], wv_ref[...], 0, 0)
    grad_ref[...] = (total + sum_ref[...] + four[...].astype(F32)).astype(BF16)


def finish(att_t, w_out, dq, dk, dv, wq_t, wk_t, wv_t, total, four):
    d, n = att_t.shape
    return pl.pallas_call(
        final_kernel,
        out_shape=(jax.ShapeDtypeStruct((n, d), BF16),) * 2,
        compiler_params=params(13),
        cost_estimate=cost(40),
        name="finish",
    )(att_t, w_out, dq, dk, dv, wq_t, wk_t, wv_t, total, four)


def added(parts, xs, total=None):
    for part, x in zip(parts, xs):
        term = dot(part[...], x[...], 1, 0)
        total = term if total is None else total + term
    return total


def early_kernel(count, *refs):
    xs, dks, dvs = refs[:count], refs[count : 2 * count], refs[2 * count : 3 * count]
    att_ref, cot_ref, g_ref = refs[3 * count :]
    g_ref[0] = added(dks, xs)
    g_ref[1] = added(dvs, xs)
    g_ref[2] = dot(cot_ref[...], att_ref[...], 0, 1)


def early_terms(xs, dks, dvs, att_t, cot):
    n, d = cot.shape
    return pl.pallas_call(
        functools.partial(early_kernel, len(xs)),
        out_shape=jax.ShapeDtypeStruct((3, d, d), F32),
        compiler_params=params(14),
        cost_estimate=cost(4),
        name="early_terms",
    )(*xs, *dks, *dvs, att_t, cot)


def weights_kernel(count, core_ref, *refs):
    xs, dks, dvs = refs[:count], refs[count : 2 * count], refs[2 * count : 3 * count]
    dq_ref, early_ref, keep_ref, give_ref, sums = refs[3 * count :]

    def keep(place, value):
        for owner in range(sums.shape[0]):
            sums[owner, 4 * place : 4 * place + 4, :] = value[4 * owner : 4 * owner + 4, :]

    keep(0, dot((dq_ref[...] * 0.125).astype(BF16), xs[0][...], 1, 0))
    keep(1, added(dks, xs, early_ref[0]))
    keep(2, added(dvs, xs, early_ref[1]))
    keep(3, early_ref[2])
    core = core_ref[0]
    for high in range(2):
        here = pl.ds(pl.multiple_of((2 * high + core) * 32, 32), 32)
        there = pl.ds(pl.multiple_of((2 * high + 1 - core) * 32, 32), 32)
        keep_ref[32 * high : 32 * high + 32] = sums[here].astype(BF16)
        give_ref[32 * high : 32 * high + 32] = sums[there].astype(BF16)


def weight_terms(core, xs, dks, dvs, dq, early):
    n, d = xs[0].shape
    half = jax.ShapeDtypeStruct((64, 16, d), BF16)
    return pl.pallas_call(
        functools.partial(weights_kernel, len(xs)),
        out_shape=(half, half),
        in_specs=[SCALAR] + [pl.BlockSpec(memory_space=pltpu.VMEM)] * (3 * len(xs) + 2),
        scratch_shapes=[pltpu.VMEM((128, 16, d), F32)],
        compiler_params=params(18),
        cost_estimate=cost(3.5),
        name="weight_terms",
    )(core, *xs, *dks, *dvs, dq, early)


def either_kernel(flag_ref, first_ref, second_ref, out_ref):
    @pl.when(flag_ref[0] > 0)
    def _():
        out_ref[...] = first_ref[...]

    @pl.when(flag_ref[0] <= 0)
    def _():
        out_ref[...] = second_ref[...]


def either(flag, first, second):
    return pl.pallas_call(
        either_kernel,
        out_shape=jax.ShapeDtypeStruct(first.shape, first.dtype),
        in_specs=[SCALAR] + [pl.BlockSpec(memory_space=pltpu.VMEM)] * 2,
        compiler_params=params(4),
        cost_estimate=cost(0.5),
        name="either",
    )(flag.astype(jnp.int32).reshape(1), first, second)


def sum_kernel(first_ref, second_ref, out_ref):
    out_ref[...] = (first_ref[...].astype(F32) + second_ref[...].astype(F32)).astype(BF16)


def sum_of(first, second):
    return pl.pallas_call(
        sum_kernel,
        out_shape=jax.ShapeDtypeStruct(first.shape, BF16),
        compiler_params=params(6),
        cost_estimate=cost(1),
        name="sum_of",
    )(first, second)


def place(z, x, y):
    return (z % 2) * 16 + (x % 4) * 4 + y % 4


def y_ring(value, step, sources=(0, 1, 2, 3)):
    pairs = [(place(z, x, y), place(z, x, y + step)) for z in range(2) for x in range(4) for y in sources]
    return lax.ppermute(value, "ctx", pairs)


def shifted(value, step):
    return lax.ppermute(
        value, "ctx", [(i, i + step) for i in range(max(0, -step), min(32, 32 - step))]
    )


def body(series, w_query, w_key, w_value, w_out, cotangent):
    x = series[0]
    cot = cotangent[0]
    n, d = x.shape
    position = lax.axis_index("ctx")
    y = position % 4
    x4 = shifted(x, 4)
    x1, x2 = shifted(x, 1), y_ring(x, 2, (0, 1))
    q_t, wq_t, wk_t, wv_t = project(x, w_query, w_key, w_value)
    order = (0, 4, 1, 16, 2, 8)
    seen = {p: (position >= p).astype(jnp.int32).reshape(1) for p in order}
    held = {0: forward(0, seen[0], x, wk_t, wv_t, q_t)}
    x4, later, _ = lax.optimization_barrier((x4, x, held[0][1]))
    x2 = either(y < 2, y_ring(x4, 2, (2, 3)), x2)
    held[4] = forward(4, seen[4], x4, wk_t, wv_t, q_t)
    latest, _ = lax.optimization_barrier((later, held[4][1]))
    x16, x8 = shifted(later, 16), shifted(latest, 8)
    blocks = {0: x, 1: x1, 2: x2, 4: x4, 8: x8, 16: x16}
    for p in order[2:]:
        held[p] = forward(p, seen[p], blocks[p], wk_t, wv_t, q_t)
    do_t, att_t, delta, *factors = join([held[p][1:4] for p in order], w_out, cot)
    factor = dict(zip(order, factors))
    dq = jnp.zeros((d, n), F32)
    dk, dv = {}, {}
    back = {}
    for p in (1, 2, 16, 8, 0, 4):
        weights, _, _, _, keys, values = held[p]
        dq, dk[p], dv[p], *sent = backward(
            p, seen[p], weights, keys, values, q_t, do_t, factor[p], delta, wk_t, wv_t, dq
        )
        if p in (1, 2):
            back[p] = y_ring(sent[0], -p)
        elif sent:
            back[p] = shifted(sent[0], -p)
    dk[1], back[1], back[2] = lax.optimization_barrier((dk[1], back[1], back[2]))
    ready = (1, 2, 8, 16)
    early = early_terms([blocks[i] for i in ready], [dk[i] for i in ready], [dv[i] for i in ready], att_t, cot)
    early, back[16] = lax.optimization_barrier((early, back[16]))
    core = lax.axis_index("dp") % 2
    kept, given = weight_terms(
        core.astype(jnp.int32).reshape(1), [x, x4], [dk[0], dk[4]], [dv[0], dv[4]], dq, early
    )
    wraps = jnp.stack([y == 3, y >= 2]).astype(jnp.int32)
    sent, total = returned(wraps, dk[4], dv[4], wk_t, wv_t, back[1], back[2], back[8], back[16])
    back[4] = shifted(sent, -4)
    given = lax.ppermute(given, "dp", [(0, 1), (1, 0), (2, 3), (3, 2)])
    terms = sum_of(kept, given)
    same_core = [[32 * i + j for i in (k, k + 2) for j in range(32)] for k in range(2)]
    terms = lax.all_to_all(terms, ("dp", "ctx"), 0, 0, axis_index_groups=same_core, tiled=True)
    grads = jnp.sum(terms.astype(F32), axis=0).reshape(4, 4, d).transpose(0, 2, 1)
    output, input_grad = finish(att_t, w_out, dq, dk[0], dv[0], wq_t, wk_t, wv_t, total, back[4])
    return (output[None], input_grad[None], grads[0], grads[1], grads[2], grads[3])


def solution(mesh):
    return jax.shard_map(
        body,
        mesh=mesh,
        in_specs=(P("dp", "ctx", None), P(), P(), P(), P(), P("dp", "ctx", None)),
        out_specs=(
            P("dp", "ctx", None),
            P("dp", "ctx", None),
            P(None, ("dp", "ctx")),
            P(None, ("dp", "ctx")),
            P(None, ("dp", "ctx")),
            P(None, ("dp", "ctx")),
        ),
        check_vma=False,
    )
```

```python
import functools

import jax
import jax.numpy as jnp
from jax import lax
from jax.experimental import pallas as pl
from jax.experimental.pallas import tpu as pltpu
from jax.sharding import PartitionSpec as P

HEADS = 8
SIZE = 64
F32 = jnp.float32
BF16 = jnp.bfloat16
LOW = -3.0e38
MIB = 2**20


def dot(left, right, left_dim, right_dim):
    return lax.dot_general(
        left, right, (((left_dim,), (right_dim,)), ((), ())), preferred_element_type=F32
    )


def whole(shape):
    return pl.BlockSpec(shape, lambda *_: (0,) * len(shape), pipeline_mode=pl.Buffered(1))


def head_rows(count, width):
    return pl.BlockSpec((count * SIZE, width), lambda h: (h, 0))


def head_stat(count, width):
    return pl.BlockSpec((count, 1, width), lambda h: (h, 0, 0))


SCALAR = pl.BlockSpec(memory_space=pltpu.SMEM)


def params(mib=16):
    return pltpu.CompilerParams(vmem_limit_bytes=mib * MIB)


def cost(microseconds):
    return pl.CostEstimate(flops=int(microseconds * 1.1e9), bytes_accessed=MIB, transcendentals=0)


def project_kernel(x_ref, wq_ref, wk_ref, wv_ref, q_ref, wq_t_ref, wk_t_ref, wv_t_ref):
    wq_t_ref[...] = wq_ref[...].T
    q_ref[...] = dot(wq_t_ref[...], x_ref[...], 1, 1).astype(BF16) * jnp.asarray(0.125, BF16)
    wk_t_ref[...] = wk_ref[...].T
    wv_t_ref[...] = wv_ref[...].T


def project(x, w_query, w_key, w_value):
    n, d = x.shape
    square = jax.ShapeDtypeStruct((d, d), BF16)
    return pl.pallas_call(
        project_kernel,
        out_shape=(jax.ShapeDtypeStruct((d, n), BF16),) + (square,) * 3,
        compiler_params=params(12),
        cost_estimate=cost(2),
        name="project",
    )(x, w_query, w_key, w_value)


def forward_kernel(own, count, seen_ref, x_ref, wk_ref, wv_ref, q_ref, p_ref, m_ref, l_ref, o_ref, k_ref, v_ref):
    step = pl.program_id(0)
    seen = seen_ref[0] > 0

    @pl.when(jnp.logical_and(seen, step == 0))
    def _():
        k_ref[...] = dot(wk_ref[...], x_ref[...], 1, 1).astype(BF16)
        v_ref[...] = dot(wv_ref[...], x_ref[...], 1, 1).astype(BF16)

    @pl.when(seen)
    def _():
        n = q_ref.shape[1]
        chunk = n // 2 if own else n
        parts = [(j, start) for j in range(count) for start in range(0, n, chunk)]
        scores = []
        for j, start in parts:
            known = start + chunk if own else n
            keys = k_ref[pl.ds(pl.multiple_of((step * count + j) * SIZE, SIZE), SIZE), :known]
            scores.append(dot(keys, q_ref[j * SIZE : (j + 1) * SIZE, start : start + chunk], 0, 0))
        for (j, start), score in zip(parts, scores):
            known = start + chunk if own else n
            cols = slice(start, start + chunk)
            if own:
                at_key = lax.broadcasted_iota(jnp.int32, score.shape, 0)
                at_query = lax.broadcasted_iota(jnp.int32, score.shape, 1) + start
                score = jnp.where(at_key <= at_query, score, LOW)
            largest = jnp.max(score, axis=0, keepdims=True)
            weights = jnp.exp(score - largest).astype(BF16)
            p_ref[j, :known, cols] = weights
            if known < n:
                p_ref[j, known:, cols] = jnp.zeros((n - known, chunk), BF16)
            values = v_ref[pl.ds(pl.multiple_of((step * count + j) * SIZE, SIZE), SIZE), :known]
            values = jnp.concatenate([values, jnp.ones((16, known), BF16)], axis=0)
            mixed = dot(values, weights, 1, 0)
            m_ref[j, :, cols] = largest
            l_ref[j, :, cols] = mixed[SIZE : SIZE + 1, :]
            o_ref[j * SIZE : (j + 1) * SIZE, cols] = mixed[:SIZE, :]

    @pl.when(jnp.logical_not(seen))
    def _():
        m_ref[...] = jnp.full(m_ref.shape, LOW, F32)
        l_ref[...] = jnp.zeros(l_ref.shape, F32)
        o_ref[...] = jnp.zeros(o_ref.shape, F32)


def forward(block, seen, x, wk_t, wv_t, q_t):
    n, d = x.shape
    own = block == 0
    count = 4 if own else 2
    return pl.pallas_call(
        functools.partial(forward_kernel, own, count),
        grid=(HEADS // count,),
        out_shape=(
            jax.ShapeDtypeStruct((HEADS, n, n), BF16),
            jax.ShapeDtypeStruct((HEADS, 1, n), F32),
            jax.ShapeDtypeStruct((HEADS, 1, n), F32),
            jax.ShapeDtypeStruct((d, n), F32),
            jax.ShapeDtypeStruct((d, n), BF16),
            jax.ShapeDtypeStruct((d, n), BF16),
        ),
        in_specs=[SCALAR, whole((n, d)), whole((d, d)), whole((d, d)), head_rows(count, n)],
        out_specs=[
            pl.BlockSpec((count, n, n), lambda h: (h, 0, 0)),
            head_stat(count, n),
            head_stat(count, n),
            head_rows(count, n),
            whole((d, n)),
            whole((d, n)),
        ],
        compiler_params=params(11),
        cost_estimate=cost(4.5 if own else 6),
        name=f"forward_{block}",
    )(seen, x, wk_t, wv_t, q_t)


def join_kernel(count, *refs):
    ms, ls, os = refs[:count], refs[count : 2 * count], refs[2 * count : 3 * count]
    wo_ref, cot_ref, do_ref, att_ref, delta_ref = refs[3 * count : 3 * count + 5]
    cs = refs[3 * count + 5 :]
    do_ref[...] = dot(wo_ref[...], cot_ref[...], 1, 1).astype(BF16)
    for head in range(HEADS):
        rows = slice(head * SIZE, (head + 1) * SIZE)
        largest = functools.reduce(jnp.maximum, [m[head] for m in ms])
        factors = [jnp.exp(m[head] - largest) for m in ms]
        total = functools.reduce(jnp.add, [f * l[head] for f, l in zip(factors, ls)])
        inverse = 1.0 / total
        mixed = None
        for f, o, c in zip(factors, os, cs):
            f = f * inverse
            c[head] = f
            term = o[rows, :] * f
            mixed = term if mixed is None else mixed + term
        attended = mixed.astype(BF16)
        att_ref[rows, :] = attended
        products = attended.astype(F32) * do_ref[rows, :].astype(F32)
        delta_ref[head] = jnp.sum(products, axis=0, keepdims=True)


def join(stats, w_out, cot):
    n, d = cot.shape
    count = len(stats)
    row = jax.ShapeDtypeStruct((HEADS, 1, n), F32)
    return pl.pallas_call(
        functools.partial(join_kernel, count),
        out_shape=(
            jax.ShapeDtypeStruct((d, n), BF16),
            jax.ShapeDtypeStruct((d, n), BF16),
            row,
        )
        + (row,) * count,
        compiler_params=params(),
        cost_estimate=cost(2.5),
        name="join",
    )(*[s[0] for s in stats], *[s[1] for s in stats], *[s[2] for s in stats], w_out, cot)


def backward_kernel(
    own, sends, seen_ref, p_ref, k_ref, v_ref, q_ref, do_ref, c_ref, delta_ref, wk_ref, wv_ref, acc_ref,
    dq_ref, dk_ref, dv_ref, *dx_refs,
):
    step = pl.program_id(0)
    count = p_ref.shape[0]
    seen = seen_ref[0] > 0

    def far_block():
        grads = []
        for j in range(count):
            rows = slice(j * SIZE, (j + 1) * SIZE)
            value_dots = dot(v_ref[rows, :], do_ref[rows, :], 0, 0)
            grads.append(p_ref[j] * (value_dots - delta_ref[j]).astype(BF16))
        for j in range(count):
            rows = slice(j * SIZE, (j + 1) * SIZE)
            out = pl.ds(pl.multiple_of((step * count + j) * SIZE, SIZE), SIZE)
            factor = c_ref[j]
            scaled_q = (q_ref[rows, :].astype(F32) * factor).astype(BF16)
            scaled_do = (do_ref[rows, :].astype(F32) * factor).astype(BF16)
            dq_ref[rows, :] = acc_ref[rows, :] + dot(k_ref[rows, :], grads[j], 1, 0) * factor
            dk_ref[out, :] = dot(scaled_q, grads[j], 1, 1).astype(BF16)
            dv_ref[out, :] = dot(scaled_do, p_ref[j], 1, 1).astype(BF16)

    def own_block():
        n = q_ref.shape[1]
        half = n // 2
        parts = ((0, half, half), (half, n, n))
        grads = []
        for j in range(count):
            rows = slice(j * SIZE, (j + 1) * SIZE)
            for start, stop, known in parts:
                value_dots = dot(v_ref[rows, :known], do_ref[rows, start:stop], 0, 0)
                delta = delta_ref[j, :, start:stop]
                grads.append(p_ref[j, :known, start:stop] * (value_dots - delta).astype(BF16))
        for j in range(count):
            rows = slice(j * SIZE, (j + 1) * SIZE)
            out = pl.ds(pl.multiple_of((step * count + j) * SIZE, SIZE), SIZE)
            dks, dvs = [], []
            for (start, stop, known), grad in zip(parts, grads[2 * j : 2 * j + 2]):
                factor = c_ref[j, :, start:stop]
                scaled_q = (q_ref[rows, start:stop].astype(F32) * factor).astype(BF16)
                scaled_do = (do_ref[rows, start:stop].astype(F32) * factor).astype(BF16)
                dq = dot(k_ref[rows, :known], grad, 1, 0) * factor
                dq_ref[rows, start:stop] = acc_ref[rows, start:stop] + dq
                dks.append(dot(scaled_q, grad, 1, 1))
                dvs.append(dot(scaled_do, p_ref[j, :known, start:stop], 1, 1))
            for ref, (first, second) in ((dk_ref, dks), (dv_ref, dvs)):
                ref[out, :half] = (first + second[:, :half]).astype(BF16)
                ref[out, half:] = second[:, half:].astype(BF16)

    pl.when(seen)(own_block if own else far_block)

    @pl.when(jnp.logical_not(seen))
    def _():
        out = pl.ds(pl.multiple_of(step * count * SIZE, count * SIZE), count * SIZE)
        dq_ref[...] = acc_ref[...]
        dk_ref[out, :] = jnp.zeros(k_ref.shape, BF16)
        dv_ref[out, :] = jnp.zeros(k_ref.shape, BF16)

    if sends:

        @pl.when(step == HEADS // count - 1)
        def _():
            total = dot(dk_ref[...], wk_ref[...], 0, 0) + dot(dv_ref[...], wv_ref[...], 0, 0)
            dx_refs[0][...] = total.astype(BF16)


def backward(block, seen, p, k, v, q_t, do_t, c, delta, wk_t, wv_t, acc):
    d, n = q_t.shape
    sends = block not in (0, 4)
    count = 4
    return pl.pallas_call(
        functools.partial(backward_kernel, block == 0, sends),
        grid=(HEADS // count,),
        out_shape=[
            jax.ShapeDtypeStruct((d, n), F32),
            jax.ShapeDtypeStruct((d, n), BF16),
            jax.ShapeDtypeStruct((d, n), BF16),
        ]
        + [jax.ShapeDtypeStruct((n, d), BF16)] * sends,
        in_specs=[
            SCALAR,
            pl.BlockSpec((count, n, n), lambda h: (h, 0, 0)),
            *[head_rows(count, n)] * 4,
            *[head_stat(count, n)] * 2,
            *[whole((d, d))] * 2,
            head_rows(count, n),
        ],
        out_specs=[head_rows(count, n), whole((d, n)), whole((d, n))] + [whole((n, d))] * sends,
        compiler_params=params(13),
        cost_estimate=cost(5.5),
        name=f"backward_{block}",
    )(seen, p, k, v, q_t, do_t, c, delta, wk_t, wv_t, acc)


def returned_kernel(flag_ref, dk_ref, dv_ref, wk_ref, wv_ref, *refs):
    one, two, eight, sixteen, sent_ref, sum_ref = refs
    total = dot(dk_ref[...], wk_ref[...], 0, 0) + dot(dv_ref[...], wv_ref[...], 0, 0)
    total = total + jnp.where(flag_ref[0] > 0, one[...], 0).astype(F32)
    total = total + jnp.where(flag_ref[1] > 0, two[...], 0).astype(F32)
    sent_ref[...] = total.astype(BF16)
    kept = eight[...].astype(F32) + sixteen[...].astype(F32)
    kept = kept + jnp.where(flag_ref[0] > 0, 0, one[...]).astype(F32)
    kept = kept + jnp.where(flag_ref[1] > 0, 0, two[...]).astype(F32)
    sum_ref[...] = kept.astype(BF16)


def returned(flags, dk, dv, wk_t, wv_t, *backs):
    d, n = dk.shape
    return pl.pallas_call(
        returned_kernel,
        out_shape=(jax.ShapeDtypeStruct((n, d), BF16),) * 2,
        in_specs=[SCALAR] + [pl.BlockSpec(memory_space=pltpu.VMEM)] * 8,
        compiler_params=params(10),
        cost_estimate=cost(20),
        name="returned",
    )(flags, dk, dv, wk_t, wv_t, *backs)


def final_kernel(att_ref, wo_ref, dq_ref, dk_ref, dv_ref, wq_ref, wk_ref, wv_ref, sum_ref, four, out_ref, grad_ref):
    out_ref[...] = dot(att_ref[...], wo_ref[...], 0, 0).astype(BF16)
    total = dot((dq_ref[...] * 0.125).astype(BF16), wq_ref[...], 0, 0)
    total = total + dot(dk_ref[...], wk_ref[...], 0, 0) + dot(dv_ref[...], wv_ref[...], 0, 0)
    grad_ref[...] = (total + sum_ref[...].astype(F32) + four[...].astype(F32)).astype(BF16)


def finish(att_t, w_out, dq, dk, dv, wq_t, wk_t, wv_t, total, four):
    d, n = att_t.shape
    return pl.pallas_call(
        final_kernel,
        out_shape=(jax.ShapeDtypeStruct((n, d), BF16),) * 2,
        compiler_params=params(13),
        cost_estimate=cost(40),
        name="finish",
    )(att_t, w_out, dq, dk, dv, wq_t, wk_t, wv_t, total, four)


def added(parts, xs, total=None):
    for part, x in zip(parts, xs):
        term = dot(part[...], x[...], 1, 0)
        total = term if total is None else total + term
    return total


def early_kernel(count, *refs):
    xs, dks, dvs = refs[:count], refs[count : 2 * count], refs[2 * count : 3 * count]
    att_ref, cot_ref, g_ref = refs[3 * count :]
    g_ref[0] = added(dks, xs)
    g_ref[1] = added(dvs, xs)
    g_ref[2] = dot(cot_ref[...], att_ref[...], 0, 1)


def early_terms(xs, dks, dvs, att_t, cot):
    n, d = cot.shape
    return pl.pallas_call(
        functools.partial(early_kernel, len(xs)),
        out_shape=jax.ShapeDtypeStruct((3, d, d), F32),
        compiler_params=params(14),
        cost_estimate=cost(4),
        name="early_terms",
    )(*xs, *dks, *dvs, att_t, cot)


def weights_kernel(count, core_ref, *refs):
    xs, dks, dvs = refs[:count], refs[count : 2 * count], refs[2 * count : 3 * count]
    dq_ref, early_ref, keep_ref, give_ref, sums = refs[3 * count :]

    def keep(place, value):
        for owner in range(sums.shape[0]):
            sums[owner, 4 * place : 4 * place + 4, :] = value[4 * owner : 4 * owner + 4, :]

    keep(0, dot((dq_ref[...] * 0.125).astype(BF16), xs[0][...], 1, 0))
    keep(1, added(dks, xs, early_ref[0]))
    keep(2, added(dvs, xs, early_ref[1]))
    keep(3, early_ref[2])
    core = core_ref[0]
    for high in range(2):
        here = pl.ds(pl.multiple_of((2 * high + core) * 32, 32), 32)
        there = pl.ds(pl.multiple_of((2 * high + 1 - core) * 32, 32), 32)
        keep_ref[32 * high : 32 * high + 32] = sums[here].astype(BF16)
        give_ref[32 * high : 32 * high + 32] = sums[there].astype(BF16)


def weight_terms(core, xs, dks, dvs, dq, early):
    n, d = xs[0].shape
    half = jax.ShapeDtypeStruct((64, 16, d), BF16)
    return pl.pallas_call(
        functools.partial(weights_kernel, len(xs)),
        out_shape=(half, half),
        in_specs=[SCALAR] + [pl.BlockSpec(memory_space=pltpu.VMEM)] * (3 * len(xs) + 2),
        scratch_shapes=[pltpu.VMEM((128, 16, d), F32)],
        compiler_params=params(18),
        cost_estimate=cost(3.5),
        name="weight_terms",
    )(core, *xs, *dks, *dvs, dq, early)


def either_kernel(flag_ref, first_ref, second_ref, out_ref):
    @pl.when(flag_ref[0] > 0)
    def _():
        out_ref[...] = first_ref[...]

    @pl.when(flag_ref[0] <= 0)
    def _():
        out_ref[...] = second_ref[...]


def either(flag, first, second):
    return pl.pallas_call(
        either_kernel,
        out_shape=jax.ShapeDtypeStruct(first.shape, first.dtype),
        in_specs=[SCALAR] + [pl.BlockSpec(memory_space=pltpu.VMEM)] * 2,
        compiler_params=params(4),
        cost_estimate=cost(0.5),
        name="either",
    )(flag.astype(jnp.int32).reshape(1), first, second)


def sum_kernel(first_ref, second_ref, out_ref):
    out_ref[...] = (first_ref[...].astype(F32) + second_ref[...].astype(F32)).astype(BF16)


def sum_of(first, second):
    return pl.pallas_call(
        sum_kernel,
        out_shape=jax.ShapeDtypeStruct(first.shape, BF16),
        compiler_params=params(6),
        cost_estimate=cost(1),
        name="sum_of",
    )(first, second)


def place(z, x, y):
    return (z % 2) * 16 + (x % 4) * 4 + y % 4


def y_ring(value, step, sources=(0, 1, 2, 3)):
    pairs = [(place(z, x, y), place(z, x, y + step)) for z in range(2) for x in range(4) for y in sources]
    return lax.ppermute(value, "ctx", pairs)


def shifted(value, step):
    return lax.ppermute(
        value, "ctx", [(i, i + step) for i in range(max(0, -step), min(32, 32 - step))]
    )


def body(series, w_query, w_key, w_value, w_out, cotangent):
    x = series[0]
    cot = cotangent[0]
    n, d = x.shape
    position = lax.axis_index("ctx")
    y = position % 4
    x4 = shifted(x, 4)
    x1, x2 = shifted(x, 1), y_ring(x, 2, (0, 1))
    q_t, wq_t, wk_t, wv_t = project(x, w_query, w_key, w_value)
    order = (0, 4, 1, 16, 2, 8)
    seen = {p: (position >= p).astype(jnp.int32).reshape(1) for p in order}
    held = {0: forward(0, seen[0], x, wk_t, wv_t, q_t)}
    x4, later, _ = lax.optimization_barrier((x4, x, held[0][1]))
    x2 = either(y < 2, y_ring(x4, 2, (2, 3)), x2)
    held[4] = forward(4, seen[4], x4, wk_t, wv_t, q_t)
    latest, _ = lax.optimization_barrier((later, held[4][1]))
    x16, x8 = shifted(later, 16), shifted(latest, 8)
    blocks = {0: x, 1: x1, 2: x2, 4: x4, 8: x8, 16: x16}
    for p in order[2:]:
        held[p] = forward(p, seen[p], blocks[p], wk_t, wv_t, q_t)
    do_t, att_t, delta, *factors = join([held[p][1:4] for p in order], w_out, cot)
    factor = dict(zip(order, factors))
    dq = jnp.zeros((d, n), F32)
    dk, dv = {}, {}
    back = {}
    for p in (1, 2, 16, 8, 0, 4):
        weights, _, _, _, keys, values = held[p]
        dq, dk[p], dv[p], *sent = backward(
            p, seen[p], weights, keys, values, q_t, do_t, factor[p], delta, wk_t, wv_t, dq
        )
        if p in (1, 2):
            back[p] = y_ring(sent[0], -p)
        elif sent:
            back[p] = shifted(sent[0], -p)
    dk[1], back[1], back[2] = lax.optimization_barrier((dk[1], back[1], back[2]))
    ready = (1, 2, 8, 16)
    early = early_terms([blocks[i] for i in ready], [dk[i] for i in ready], [dv[i] for i in ready], att_t, cot)
    early, back[16] = lax.optimization_barrier((early, back[16]))
    core = lax.axis_index("dp") % 2
    kept, given = weight_terms(
        core.astype(jnp.int32).reshape(1), [x, x4], [dk[0], dk[4]], [dv[0], dv[4]], dq, early
    )
    wraps = jnp.stack([y == 3, y >= 2]).astype(jnp.int32)
    sent, total = returned(wraps, dk[4], dv[4], wk_t, wv_t, back[1], back[2], back[8], back[16])
    back[4] = shifted(sent, -4)
    given = lax.ppermute(given, "dp", [(0, 1), (1, 0), (2, 3), (3, 2)])
    terms = sum_of(kept, given)
    same_core = [[32 * i + j for i in (k, k + 2) for j in range(32)] for k in range(2)]
    terms = lax.all_to_all(terms, ("dp", "ctx"), 0, 0, axis_index_groups=same_core, tiled=True)
    grads = jnp.sum(terms.astype(F32), axis=0).reshape(4, 4, d).transpose(0, 2, 1)
    output, input_grad = finish(att_t, w_out, dq, dk[0], dv[0], wq_t, wk_t, wv_t, total, back[4])
    return (output[None], input_grad[None], grads[0], grads[1], grads[2], grads[3])


def solution(mesh):
    return jax.shard_map(
        body,
        mesh=mesh,
        in_specs=(P("dp", "ctx", None), P(), P(), P(), P(), P("dp", "ctx", None)),
        out_specs=(
            P("dp", "ctx", None),
            P("dp", "ctx", None),
            P(None, ("dp", "ctx")),
            P(None, ("dp", "ctx")),
            P(None, ("dp", "ctx")),
            P(None, ("dp", "ctx")),
        ),
        check_vma=False,
    )
```
